32 devices in a mesh: slide: 2 (over x), seq: 16 (over z, y, core).
Axes of the slice: x: 2, y: 2, z: 4, core: 2. Of those that a mesh axis runs over, the one named last changes fastest.
Arguments:
- tile_embed: bfloat16 [4096, 768], P(('slide', 'seq')), parts along dimension 0, may hold values from -8 to 8
- grad_output: bfloat16 [4096, 768], P(('slide', 'seq')), parts along dimension 0, may hold values from -6 to 6
- query_key_value_weight: bfloat16 [768, 2304], replicated, may hold values from -0.5 to 0.5
- conv_weight: float32 [9, 768], replicated, may hold values from -2.5 to 2.5
- neighbours: int32 [9, 4096], P(None, ('slide', 'seq')), parts along dimension 1, may hold values from -1 to 2047, as said below
Outputs:
- attended: bfloat16 [4096, 768], P(('slide', 'seq')), parts along dimension 0
- grad_tiles: bfloat16 [4096, 768], P(('slide', 'seq')), parts along dimension 0
- grad_conv: float32 [18, 768], P('slide'), parts along dimension 0
The draws below stay inside these ranges and needn't reach their ends.
There are 2 independent parts, one for each index of `slide`. The reference program is written for one: setup_inputs(seed, part) draws one part's arguments, and reference() takes and returns one part's arrays. A program takes and returns all parts, laid end to end along the dimension named above; an argument that names none is the same for every part. Nothing has to cross between parts.
Inputs may be any that keep to these rules, and one draw needn't show every extreme that they name: Tiles are the tissue cells of a grid of 64 columns numbered in snake order. neighbours[k, i] is the tile at grid offset (k // 3 - 1, k % 3 - 1) from tile i, or -1 where that cell is outside the grid or background; neighbours[4, i] = i, and neighbours[8 - k, neighbours[k, i]] = i. Every neighbour lies within 127 positions of its tile, and some lies exactly 127 away.
All inputs are finite; a program needn't handle non-finite values.
Results may differ from the reference program's by a relative error of at most 0.012.
The reference program's roundings to bfloat16 on the way count: a program that leaves them out, or rounds other values in their place, can miss the bound.
Values may be sent and summed in bfloat16 or wider, within the bound.
A program may use at most 128 MiB of HBM per device.

```python
import math
import jax
import jax.numpy as jnp
from jax import lax

MODEL_WIDTH = 768
HEAD_COUNT = 16
HEAD_SIZE = 48
DILATION_STEP = 4
KERNEL = 9
GRID_W = 64
TOKENS = 2048
KEYS = 512
HOLES = 256


def draw_tile_embed(key, part):
    key = jax.random.fold_in(key, 7)
    second = jax.random.fold_in(key, 1)
    values = jax.random.normal(second, (TOKENS, MODEL_WIDTH), jnp.float32)
    return jnp.clip(values, -8.0, 8.0).astype(jnp.bfloat16)


def draw_query_key_value_weight(key, part):
    key = jax.random.fold_in(key, 5)
    first, second, third = jax.random.split(key, 3)
    width = 1.0 / math.sqrt(MODEL_WIDTH)
    query_part = jax.random.normal(first, (MODEL_WIDTH, MODEL_WIDTH), jnp.float32) * (1.2 * width)
    key_part = jax.random.normal(second, (MODEL_WIDTH, MODEL_WIDTH), jnp.float32) * (1.2 * width)
    value_part = jax.random.normal(third, (MODEL_WIDTH, MODEL_WIDTH), jnp.float32) * width
    joined = jnp.concatenate([query_part, key_part, value_part], axis=1)
    return jnp.clip(joined, -0.5, 0.5).astype(jnp.bfloat16)


def draw_neighbours(key, part):
    key = jax.random.fold_in(key, 11)
    cells = TOKENS + HOLES
    order = jax.random.permutation(key, cells - 2 * GRID_W).astype(jnp.int32)
    holes = jnp.zeros((cells,), jnp.int32).at[order[:HOLES] + 2 * GRID_W].set(1)
    tissue = 1 - holes
    rank = (jnp.cumsum(tissue) - 1).astype(jnp.int32)
    cell_of = jnp.nonzero(tissue, size=TOKENS)[0].astype(jnp.int32)
    row_of = cell_of // GRID_W
    within = cell_of % GRID_W
    column = jnp.where(row_of % 2 == 0, within, GRID_W - 1 - within)
    lists = []
    for k in range(9):
        row_two = row_of + (k // 3 - 1)
        col_two = column + (k % 3 - 1)
        inside = (row_two >= 0) & (col_two >= 0) & (col_two < GRID_W)
        place = jnp.where(row_two % 2 == 0, col_two, GRID_W - 1 - col_two)
        target = row_two * GRID_W + place
        inside = inside & (target < cells)
        clipped = jnp.clip(target, 0, cells - 1)
        usable = inside & (tissue[clipped] == 1)
        lists.append(jnp.where(usable, rank[clipped], -1))
    return jnp.stack(lists).astype(jnp.int32)


def levels(stream_key, shape, cuts, smallest, largest):
    def one(dim, parts):
        steps = jax.random.uniform(jax.random.fold_in(jax.random.fold_in(stream_key, 6), dim), (parts,), jnp.float32, smallest / len(cuts), largest / len(cuts))
        return jnp.repeat(jnp.exp(steps), shape[dim] // parts).reshape((-1,) + (1,) * (len(shape) - dim - 1))

    level = one(*cuts[0])
    for cut in cuts[1:]:
        level = level * one(*cut)
    return level


def normal_values(rng, extent, deviation, most, pieces=(), kind=jnp.bfloat16):
    values = deviation * jax.random.normal(rng, extent, jnp.float32)
    if pieces:
        values = values * levels(rng, extent, pieces, -0.22, 0.18)
    return jnp.clip(values, -most, most).astype(kind)


def setup_inputs(seed: int = 0, part: int = 0) -> dict:
    key_of = jax.random.split(jax.random.key(seed), 6)
    own_keys = jax.random.split(jax.random.fold_in(key_of[5], part), 6)
    return {
        "tile_embed": draw_tile_embed(jax.random.fold_in(jax.random.fold_in(key_of[5], part), 71), part),
        "grad_output": normal_values(own_keys[1], (TOKENS, MODEL_WIDTH), 1.0, 6.0, ((0, 16),)),
        "query_key_value_weight": draw_query_key_value_weight(jax.random.fold_in(key_of[5], 71), part),
        "conv_weight": normal_values(key_of[3], (KERNEL, MODEL_WIDTH), 0.3, 2.5, (), jnp.float32),
        "neighbours": draw_neighbours(jax.random.fold_in(jax.random.fold_in(key_of[5], part), 71), part),
    }


def select_dilated(full_result, item_count):
    each_group = HEAD_COUNT // DILATION_STEP
    five_value = full_result.reshape(item_count // DILATION_STEP, DILATION_STEP, each_group, DILATION_STEP, HEAD_SIZE)
    return jnp.stack([five_value[:, residue_index, :, residue_index, :] for residue_index in range(DILATION_STEP)], axis=2).reshape(item_count // DILATION_STEP, MODEL_WIDTH)


def spread_dilated(selected_rows):
    item_count = selected_rows.shape[0]
    five_value = selected_rows.reshape(item_count, 1, HEAD_COUNT // DILATION_STEP, DILATION_STEP, HEAD_SIZE)
    unit_vector = jnp.eye(DILATION_STEP, dtype=selected_rows.dtype).reshape(1, DILATION_STEP, 1, DILATION_STEP, 1)
    return (five_value * unit_vector).reshape(item_count * DILATION_STEP, MODEL_WIDTH)


def heads_first(values):
    return jnp.transpose(values.reshape(KEYS, HEAD_COUNT, HEAD_SIZE), (1, 0, 2))


def heads_back(values):
    return spread_dilated(jnp.transpose(values, (1, 0, 2)).reshape(KEYS, MODEL_WIDTH))


def head_pass(items):
    queries, keys, values, douts = items
    scale = HEAD_SIZE ** -0.5
    scores = jnp.dot(queries, keys.T, preferred_element_type=jnp.float32) * scale
    top = jnp.max(scores, axis=1, keepdims=True)
    log_total = top + jnp.log(jnp.sum(jnp.exp(scores - top), axis=1, keepdims=True))
    weights = jnp.exp(scores - log_total)
    weights_low = weights.astype(jnp.bfloat16)
    output = jnp.dot(weights_low, values, preferred_element_type=jnp.float32).astype(jnp.bfloat16)
    delta = jnp.sum(douts.astype(jnp.float32) * output.astype(jnp.float32), axis=1, keepdims=True)
    dprob = jnp.dot(douts, values.T, preferred_element_type=jnp.float32)
    dscore = (weights * (dprob - delta) * scale).astype(jnp.bfloat16)
    grad_q = jnp.dot(dscore, keys, preferred_element_type=jnp.float32).astype(jnp.bfloat16)
    grad_k = jnp.dot(dscore.T, queries, preferred_element_type=jnp.float32).astype(jnp.bfloat16)
    grad_v = jnp.dot(weights_low.T, douts, preferred_element_type=jnp.float32).astype(jnp.bfloat16)
    return output, grad_q, grad_k, grad_v


def reference(tile_embed, grad_output, query_key_value_weight, conv_weight, neighbours):
    valid = neighbours >= 0
    index = jnp.where(valid, neighbours, TOKENS).astype(jnp.int32)
    padded = jnp.concatenate([tile_embed, jnp.zeros((1, MODEL_WIDTH), tile_embed.dtype)], axis=0)
    summed = tile_embed.astype(jnp.float32)
    for k in range(KERNEL):
        summed = summed + conv_weight[k][None, :] * padded[index[k]].astype(jnp.float32)
    mixed_tiles = summed.astype(jnp.bfloat16)
    projected = jnp.dot(mixed_tiles, query_key_value_weight, preferred_element_type=jnp.float32).astype(jnp.bfloat16)
    queries = heads_first(select_dilated(projected[:, :MODEL_WIDTH], TOKENS))
    keys = heads_first(select_dilated(projected[:, MODEL_WIDTH:2 * MODEL_WIDTH], TOKENS))
    values = heads_first(select_dilated(projected[:, 2 * MODEL_WIDTH:], TOKENS))
    douts = heads_first(select_dilated(grad_output, TOKENS))
    output, grad_q, grad_k, grad_v = lax.map(head_pass, (queries, keys, values, douts))
    attended = heads_back(output)
    dproj = jnp.concatenate([heads_back(grad_q), heads_back(grad_k), heads_back(grad_v)], axis=1)
    dmixed = lax.dot_general(dproj, query_key_value_weight, (((1,), (1,)), ((), ())), preferred_element_type=jnp.float32)
    grad_conv = jnp.stack([jnp.sum(dmixed * padded[index[k]].astype(jnp.float32), axis=0) for k in range(KERNEL)])
    total = jnp.zeros((TOKENS + 1, MODEL_WIDTH), jnp.float32)
    for k in range(KERNEL):
        total = total.at[index[k]].add(conv_weight[k][None, :] * dmixed)
    grad_tiles = (dmixed + total[:TOKENS]).astype(jnp.bfloat16)
    return attended, grad_tiles, grad_conv
```

```python
import functools

import jax
import jax.numpy as jnp
from jax import lax
from jax.experimental import pallas as pl
from jax.experimental.pallas import tpu as pltpu
from jax.sharding import PartitionSpec as P

MODEL_WIDTH = 768
HEAD_COUNT = 16
HEAD_SIZE = 48
DILATION_STEP = 4
KERNEL = 9
REACH = 127


def extended_2(shard, sides, width):
    for axis, dim in sides:
        count, length = (lax.axis_size(axis), shard.shape[dim])
        up = [(i, (i + 1) % count) for i in range(count - 1)]
        down = [(j, i) for i, j in up]
        last = lax.slice_in_dim(shard, length - width, length, axis=dim)
        leading = lax.slice_in_dim(shard, 0, width, axis=dim)
        before = lax.ppermute(last, axis, up)
        after = lax.ppermute(leading, axis, down)
        shard = jnp.concatenate([before, shard, after], axis=dim)
    return shard


def from_behind(value, axis, steps):
    count = lax.axis_size(axis)
    leading, last = (max(0, -steps), min(count, count - steps))
    return lax.ppermute(value, axis, [(source, source + steps) for source in range(leading, last)])


def select_dilated(full_result, item_count):
    each_group = HEAD_COUNT // DILATION_STEP
    five_value = full_result.reshape(
        item_count // DILATION_STEP, DILATION_STEP, each_group, DILATION_STEP, HEAD_SIZE
    )
    return jnp.stack(
        [
            five_value[:, residue_index, :, residue_index, :]
            for residue_index in range(DILATION_STEP)
        ],
        axis=2,
    ).reshape(item_count // DILATION_STEP, MODEL_WIDTH)


def spread_dilated(selected_rows):
    item_count = selected_rows.shape[0]
    five_value = selected_rows.reshape(
        item_count, 1, HEAD_COUNT // DILATION_STEP, DILATION_STEP, HEAD_SIZE
    )
    unit_vector = jnp.eye(DILATION_STEP, dtype=selected_rows.dtype).reshape(
        1, DILATION_STEP, 1, DILATION_STEP, 1
    )
    return (five_value * unit_vector).reshape(item_count * DILATION_STEP, MODEL_WIDTH)


def contract_last(left, right):
    return lax.dot_general(
        left, right, (((1,), (1,)), ((), ())), preferred_element_type=jnp.float32
    )


def contract_first(left, right):
    return lax.dot_general(
        left, right, (((0,), (0,)), ((), ())), preferred_element_type=jnp.float32
    )


def head_forward(items):
    queries, keys, values, douts = items
    scale = HEAD_SIZE ** (-0.5)
    scores = contract_last(queries, keys) * scale
    top = jnp.max(scores, axis=1, keepdims=True)
    log_total = top + jnp.log(jnp.sum(jnp.exp(scores - top), axis=1, keepdims=True))
    weights = jnp.exp(scores - log_total)
    weights_low = weights.astype(jnp.bfloat16)
    output = jnp.dot(weights_low, values, preferred_element_type=jnp.float32).astype(jnp.bfloat16)
    delta = jnp.sum(douts.astype(jnp.float32) * output.astype(jnp.float32), axis=1)
    dprob = contract_last(douts, values)
    dscore = (weights * (dprob - delta[:, None]) * scale).astype(jnp.bfloat16)
    grad_q = jnp.dot(dscore, keys, preferred_element_type=jnp.float32).astype(jnp.bfloat16)
    return (output, log_total[:, 0], delta, grad_q)


def head_keyside(items):
    query_piece, dout_piece, lse_piece, delta_piece, local_keys, local_values = items
    scale = HEAD_SIZE ** (-0.5)
    piece_scores = contract_last(query_piece, local_keys) * scale
    piece_weights = jnp.exp(piece_scores - lse_piece[:, None])
    value_part = contract_first(piece_weights.astype(jnp.bfloat16), dout_piece)
    piece_dprob = contract_last(dout_piece, local_values)
    piece_dscore = (piece_weights * (piece_dprob - delta_piece[:, None]) * scale).astype(
        jnp.bfloat16
    )
    key_part = contract_first(piece_dscore, query_piece)
    return (key_part, value_part)


def heads_lead(values, item_count):
    return jnp.transpose(values.reshape(item_count, HEAD_COUNT, HEAD_SIZE), (1, 0, 2))


def per_device(tile_embed, grad_output, query_key_value_weight, conv_weight, neighbours):
    count_of_rows = tile_embed.shape[0]
    partial_rows = count_of_rows // DILATION_STEP
    each_group = HEAD_COUNT // DILATION_STEP
    extended = extended_2(tile_embed, (("seq", 0),), REACH)
    valid = neighbours >= 0
    offset = lax.axis_index("seq") * count_of_rows - REACH
    local_index = jnp.where(valid, neighbours - offset, 0)
    valid_mask = valid.astype(jnp.float32)
    near_rows = [
        extended[local_index[k]].astype(jnp.float32) * valid_mask[k][:, None] for k in range(KERNEL)
    ]
    summed = tile_embed.astype(jnp.float32)
    for k in range(KERNEL):
        summed = summed + conv_weight[k][None, :] * near_rows[k]
    mixed_tiles = summed.astype(jnp.bfloat16)
    split_weights = query_key_value_weight.reshape(
        MODEL_WIDTH, 3, each_group, DILATION_STEP, HEAD_SIZE
    )
    per_residue_class = mixed_tiles.reshape(partial_rows, DILATION_STEP, MODEL_WIDTH)
    residue_weights = [
        split_weights[:, :, :, residue_index, :].reshape(MODEL_WIDTH, 3 * each_group * HEAD_SIZE)
        for residue_index in range(DILATION_STEP)
    ]
    projected = jnp.stack(
        [
            jnp.dot(
                per_residue_class[:, residue_index, :],
                residue_weights[residue_index],
                preferred_element_type=jnp.float32,
            )
            .astype(jnp.bfloat16)
            .reshape(partial_rows, 3, each_group, HEAD_SIZE)
            for residue_index in range(DILATION_STEP)
        ],
        axis=3,
    )
    query_sel = projected[:, 0].reshape(partial_rows, MODEL_WIDTH)
    key_sel = projected[:, 1].reshape(partial_rows, MODEL_WIDTH)
    value_sel = projected[:, 2].reshape(partial_rows, MODEL_WIDTH)
    dout_sel = select_dilated(grad_output, count_of_rows)
    key_all, value_all = (
        lax.all_gather(key_sel, "seq", axis=0, tiled=True),
        lax.all_gather(value_sel, "seq", axis=0, tiled=True),
    )
    total_keys = key_all.shape[0]
    output_h, lse_h, delta_h, grad_q_h = lax.map(
        head_forward,
        (
            heads_lead(query_sel, partial_rows),
            heads_lead(key_all, total_keys),
            heads_lead(value_all, total_keys),
            heads_lead(dout_sel, partial_rows),
        ),
    )
    grad_q = jnp.transpose(grad_q_h, (1, 0, 2)).reshape(partial_rows, MODEL_WIDTH)
    output_sel = jnp.transpose(output_h, (1, 0, 2)).reshape(partial_rows, MODEL_WIDTH)
    lse_all, delta_all = (
        lax.all_gather(lse_h.T, "seq", axis=0, tiled=True),
        lax.all_gather(delta_h.T, "seq", axis=0, tiled=True),
    )
    local_keys_h = heads_lead(key_sel, partial_rows)
    local_values_h = heads_lead(value_sel, partial_rows)
    query_piece = lax.all_gather(query_sel, "seq", axis=0, tiled=True)
    dout_piece = lax.all_gather(dout_sel, "seq", axis=0, tiled=True)
    item_count = query_piece.shape[0]
    key_part, value_part = lax.map(
        head_keyside,
        (
            heads_lead(query_piece, item_count),
            heads_lead(dout_piece, item_count),
            lse_all.T,
            delta_all.T,
            local_keys_h,
            local_values_h,
        ),
    )
    grad_k = (
        jnp.transpose(key_part, (1, 0, 2)).reshape(partial_rows, MODEL_WIDTH).astype(jnp.bfloat16)
    )
    grad_v = (
        jnp.transpose(value_part, (1, 0, 2)).reshape(partial_rows, MODEL_WIDTH).astype(jnp.bfloat16)
    )
    attended = spread_dilated(output_sel)
    gradient_list = (grad_q, grad_k, grad_v)
    dmixed_parts = []
    for residue_index in range(DILATION_STEP):
        stacked = jnp.stack(
            [
                group_index.reshape(partial_rows, each_group, DILATION_STEP, HEAD_SIZE)[
                    :, :, residue_index, :
                ]
                for group_index in gradient_list
            ],
            axis=1,
        )
        dmixed_parts.append(
            contract_last(
                stacked.reshape(partial_rows, 3 * each_group * HEAD_SIZE),
                residue_weights[residue_index],
            )
        )
    dmixed = jnp.stack(dmixed_parts, axis=1).reshape(count_of_rows, MODEL_WIDTH)
    conv_terms = jnp.stack([jnp.sum(dmixed * near_rows[k], axis=0) for k in range(KERNEL)])
    grad_conv = lax.psum(conv_terms, "seq")
    contrib = jnp.zeros((count_of_rows + 2 * REACH, MODEL_WIDTH), jnp.float32)
    for k in range(KERNEL):
        contrib = contrib.at[local_index[k]].add(
            conv_weight[k][None, :] * dmixed * valid_mask[k][:, None]
        )
    from_above = from_behind(contrib[:REACH], "seq", -1)
    from_below = from_behind(
        contrib[REACH + count_of_rows :].astype(jnp.bfloat16), "seq", 1
    ).astype(jnp.float32)
    total = dmixed + contrib[REACH : REACH + count_of_rows]
    total = total + jnp.pad(from_below, ((0, count_of_rows - REACH), (0, 0)))
    total = total + jnp.pad(from_above, ((count_of_rows - REACH, 0), (0, 0)))
    grad_tiles = total.astype(jnp.bfloat16)
    return (attended, grad_tiles, grad_conv)


ROWS = 128
PART = ROWS // DILATION_STEP
PACKED = 48
LANES = 128
CHUNKS = MODEL_WIDTH // LANES
VMEM_BYTES = 56 * 1024 * 1024


def bf16_dot(left, right):
    return jnp.dot(left, right, preferred_element_type=jnp.float32)


def one_hot(column, positions):
    return jnp.where(column == positions, 1.0, 0.0).astype(jnp.bfloat16)


def remote(source, target, send_sem, recv_sem, peer):
    return pltpu.make_async_remote_copy(
        src_ref=source,
        dst_ref=target,
        send_sem=send_sem,
        recv_sem=recv_sem,
        device_id={"seq": peer},
        device_id_type=pl.DeviceIdType.MESH,
    )


def slide_kernel(
    n,
    tile_ref,
    dout_ref,
    weight_hbm,
    conv_ref,
    near_ref,
    attended_ref,
    tiles_ref,
    taps_ref,
    weight,
    near_pad,
    columns,
    columns_perm,
    halo,
    gathered_own,
    gathered,
    hot_own,
    hot_halo,
    back_own,
    back_halo,
    dout_perm,
    heads_out,
    heads_in,
    grads_out,
    grads_in,
    split,
    back_rows,
    tap_part,
    tap_in,
    tap_all,
    weight_sem,
    halo_s,
    halo_r,
    heads_s,
    heads_r,
    grads_s,
    grads_r,
    back_s,
    back_r,
    tap_s,
    tap_r,
    all_s,
    all_r,
):
    me = lax.axis_index("seq")
    load_weight = pltpu.make_async_copy(weight_hbm, weight, weight_sem)
    load_weight.start()

    barrier = pltpu.get_barrier_semaphore()

    @pl.loop(1, n)
    def _(step):
        pl.semaphore_signal(
            barrier,
            inc=1,
            device_id={"seq": lax.rem(me + step, n)},
            device_id_type=pl.DeviceIdType.MESH,
        )

    near = near_ref[...]
    near_pad[...] = jnp.full((LANES, ROWS), -1, jnp.int32)
    near_pad[0:KERNEL, :] = jnp.where(near >= 0, near - (me - 1) * ROWS, -1)
    columns[...] = near_pad[...].T
    for r in range(DILATION_STEP):
        columns_perm[r * PART : (r + 1) * PART, :] = columns[pl.ds(r, PART, stride=DILATION_STEP), :]
    lane = lax.broadcasted_iota(jnp.int32, (ROWS, ROWS), 1)
    row = lax.broadcasted_iota(jnp.int32, (ROWS, ROWS), 0)
    tile_of_lane = (lane % PART) * DILATION_STEP + lane // PART
    tile_of_row = (row % PART) * DILATION_STEP + row // PART
    for k in range(KERNEL):
        column = columns_perm[:, k : k + 1]
        rows = slice(k * ROWS, (k + 1) * ROWS)
        hot_own[rows, :] = one_hot(column, lane + ROWS)
        hot_halo[rows, 0:ROWS] = one_hot(column, lane)
        hot_halo[rows, ROWS : 2 * ROWS] = one_hot(column, lane + 2 * ROWS)
    to_perm = one_hot(tile_of_row, lane)
    dout_perm[...] = bf16_dot(to_perm, dout_ref[...]).astype(jnp.bfloat16)

    pl.semaphore_wait(barrier, n - 1)

    def exchange(source, target, send_sem, recv_sem):
        up = remote(source, target.at[pl.ds(0, ROWS)], send_sem.at[0], recv_sem.at[0], me + 1)
        down = remote(source, target.at[pl.ds(ROWS, ROWS)], send_sem.at[1], recv_sem.at[1], me - 1)
        return up, down

    def start_exchange(copies):
        pl.when(me < n - 1)(copies[0].start)
        pl.when(me > 0)(copies[1].start)

    def arrive_exchange(copies):
        pl.when(me > 0)(copies[0].wait_recv)
        pl.when(me < n - 1)(copies[1].wait_recv)

    def finish_exchange(copies):
        pl.when(me < n - 1)(copies[0].wait_send)
        pl.when(me > 0)(copies[1].wait_send)

    def clear_ends(target):
        @pl.when(me == 0)
        def _():
            target[0:ROWS, :] = jnp.zeros((ROWS, MODEL_WIDTH), jnp.bfloat16)

        @pl.when(me == n - 1)
        def _():
            target[ROWS : 2 * ROWS, :] = jnp.zeros((ROWS, MODEL_WIDTH), jnp.bfloat16)

    tile_copies = exchange(tile_ref, halo, halo_s, halo_r)
    start_exchange(tile_copies)
    clear_ends(halo)
    clear_ends(back_rows)
    gathered_own[...] = bf16_dot(hot_own[...], tile_ref[...])
    for h in range(HEAD_COUNT):
        r = h % DILATION_STEP
        piece = dout_perm[r * PART : (r + 1) * PART, h * HEAD_SIZE : (h + 1) * HEAD_SIZE]
        heads_out[h, PART:PACKED, 32:80] = piece[0:16]
        heads_out[h, PART:PACKED, 80:128] = piece[16:32]
    for k in range(KERNEL):
        column = columns[:, k : k + 1]
        rows = slice(k * ROWS, (k + 1) * ROWS)
        own = one_hot(column, tile_of_lane + ROWS)
        back_own[rows, 0:ROWS] = own
        back_own[rows, ROWS : 2 * ROWS] = own
        back_halo[rows, 0:ROWS] = one_hot(column, tile_of_lane)
        back_halo[rows, ROWS : 2 * ROWS] = one_hot(column, tile_of_lane + 2 * ROWS)

    arrive_exchange(tile_copies)
    gathered[...] = (gathered_own[...] + bf16_dot(hot_halo[...], halo[...])).astype(jnp.bfloat16)

    def tap_rows(k):
        return gathered[k * ROWS : (k + 1) * ROWS, :].astype(jnp.float32)

    summed = tap_rows(KERNEL // 2)
    for k in range(KERNEL):
        summed = summed + conv_ref[k : k + 1, :] * tap_rows(k)
    mixed = summed.astype(jnp.bfloat16)

    load_weight.wait()
    projected = [
        bf16_dot(mixed, weight[:, s * MODEL_WIDTH : (s + 1) * MODEL_WIDTH]).astype(jnp.bfloat16)
        for s in range(3)
    ]
    for h in range(HEAD_COUNT):
        r = h % DILATION_STEP
        q, k, v = [
            x[r * PART : (r + 1) * PART, h * HEAD_SIZE : (h + 1) * HEAD_SIZE] for x in projected
        ]
        heads_out[h, 0:PART, :] = jnp.concatenate([q, k, v[:, 0:32]], axis=1)
        heads_out[h, PART:PACKED, 0:16] = v[0:16, 32:48]
        heads_out[h, PART:PACKED, 16:32] = v[16:32, 32:48]

    def all_to_all(source, target, send_sem, recv_sem):
        @pl.loop(1, n)
        def _(step):
            peer = lax.rem(me + step, n)
            remote(
                source.at[peer], target.at[me], send_sem.at[peer], recv_sem.at[me], peer
            ).start()

        target[me] = source[me]

        @pl.loop(1, n)
        def _(step):
            peer = lax.rem(me + n - step, n)
            remote(
                source.at[peer], target.at[peer], send_sem.at[peer], recv_sem.at[peer], peer
            ).wait_recv()

    def finish_all_to_all(source, target, send_sem, recv_sem):
        @pl.loop(1, n)
        def _(step):
            peer = lax.rem(me + step, n)
            remote(
                source.at[peer], target.at[me], send_sem.at[peer], recv_sem.at[me], peer
            ).wait_send()

    all_to_all(heads_out, heads_in, heads_s, heads_r)

    keys_total = n * PART
    front = heads_in[:, 0:PART, :].reshape(keys_total, LANES)
    rest = heads_in[:, PART:PACKED, :]
    q = front[:, 0:48]
    k = front[:, 48:96]
    v_tail = jnp.concatenate([rest[:, :, 0:16], rest[:, :, 16:32]], axis=1).reshape(keys_total, 16)
    v = jnp.concatenate([front[:, 96:128], v_tail], axis=1)
    do = jnp.concatenate([rest[:, :, 32:80], rest[:, :, 80:128]], axis=1).reshape(keys_total, 48)
    scale = HEAD_SIZE ** (-0.5)
    scores = contract_last(k, q) * scale
    top = jnp.max(scores, axis=0, keepdims=True)
    grown = jnp.exp(scores - top)
    prob = grown * (1.0 / jnp.sum(grown, axis=0, keepdims=True))
    prob_low = prob.astype(jnp.bfloat16)
    out_t = bf16_dot(v.T, prob_low).astype(jnp.bfloat16)
    delta = jnp.sum(
        do.T.astype(jnp.float32) * out_t.astype(jnp.float32), axis=0, keepdims=True
    )
    dprob = contract_last(v, do)
    dscore = (prob * (dprob - delta) * scale).astype(jnp.bfloat16)
    out = out_t.T
    dq = bf16_dot(k.T, dscore).astype(jnp.bfloat16).T
    dk = bf16_dot(dscore, q).astype(jnp.bfloat16)
    dv = bf16_dot(prob_low, do).astype(jnp.bfloat16)
    grads_out[:, 0:PART, :] = jnp.concatenate([out, dq, dk[:, 0:32]], axis=1).reshape(
        n, PART, LANES
    )
    dk_tail = dk[:, 32:48].reshape(n, PART, 16)
    dv_rows = dv.reshape(n, PART, HEAD_SIZE)
    grads_out[:, PART:PACKED, :] = jnp.concatenate(
        [dk_tail[:, 0:16], dk_tail[:, 16:32], dv_rows[:, 0:16], dv_rows[:, 16:32]], axis=2
    )
    all_to_all(grads_out, grads_in, grads_s, grads_r)

    blank = jnp.zeros((PART, HEAD_SIZE), jnp.bfloat16)
    grown_rows = [[], [], [], []]
    for r in range(DILATION_STEP):
        lists = [[], [], [], []]
        for h in range(HEAD_COUNT):
            if h % DILATION_STEP != r:
                for entry in lists:
                    entry.append(blank)
                continue
            x = grads_in[h, 0:PART, :]
            y = grads_in[h, PART:PACKED, :]
            lists[0].append(x[:, 0:48])
            lists[1].append(x[:, 48:96])
            tail = jnp.concatenate([y[:, 0:16], y[:, 16:32]], axis=0)
            lists[2].append(jnp.concatenate([x[:, 96:128], tail], axis=1))
            lists[3].append(jnp.concatenate([y[:, 32:80], y[:, 80:128]], axis=0))
        for s in range(4):
            grown_rows[s].append(jnp.concatenate(lists[s], axis=1))
    out_perm, dq_perm, dk_perm, dv_perm = [jnp.concatenate(x, axis=0) for x in grown_rows]
    dmixed = jnp.zeros((ROWS, MODEL_WIDTH), jnp.float32)
    for s, part in enumerate((dq_perm, dk_perm, dv_perm)):
        dmixed = dmixed + contract_last(part, weight[:, s * MODEL_WIDTH : (s + 1) * MODEL_WIDTH])
    high = dmixed.astype(jnp.bfloat16)
    split[0:ROWS, :] = high
    split[ROWS : 2 * ROWS, :] = (dmixed - high.astype(jnp.float32)).astype(jnp.bfloat16)
    back_copies = exchange(split.at[pl.ds(0, ROWS)], back_rows, back_s, back_r)
    start_exchange(back_copies)

    tap_part[...] = jnp.zeros_like(tap_part)
    for k in range(KERNEL):
        term = jnp.sum(dmixed * tap_rows(k), axis=0, keepdims=True)
        for c in range(CHUNKS):
            tap_part[c, k : k + 1, :] = term[:, c * LANES : (c + 1) * LANES]
    tap_copies = [
        remote(tap_part.at[c], tap_in.at[me], tap_s.at[c], tap_r.at[me], c) for c in range(CHUNKS)
    ]
    for c in range(CHUNKS):
        pl.when(me != c)(tap_copies[c].start)

    natural = one_hot(row, tile_of_lane)
    attended_ref[...] = bf16_dot(natural, out_perm).astype(jnp.bfloat16)
    own_back = bf16_dot(back_own[...], split[...])
    total = own_back[(KERNEL // 2) * ROWS : (KERNEL // 2 + 1) * ROWS]
    for k in range(KERNEL):
        j = KERNEL - 1 - k
        total = total + conv_ref[k : k + 1, :] * own_back[j * ROWS : (j + 1) * ROWS]

    @pl.when(me < CHUNKS)
    def _():
        tap_in[me] = tap_part[me]

        @pl.loop(1, n)
        def _(step):
            peer = lax.rem(me + n - step, n)
            remote(tap_part.at[0], tap_in.at[peer], tap_s.at[0], tap_r.at[peer], peer).wait_recv()

        tap_all[me] = jnp.sum(tap_in[...], axis=0)

        @pl.loop(1, n)
        def _(step):
            peer = lax.rem(me + step, n)
            remote(tap_all.at[me], tap_all.at[me], all_s.at[peer], all_r.at[me], peer).start()

    arrive_exchange(back_copies)
    halo_back = bf16_dot(back_halo[...], back_rows[...])
    for k in range(KERNEL):
        j = KERNEL - 1 - k
        total = total + conv_ref[k : k + 1, :] * halo_back[j * ROWS : (j + 1) * ROWS]
    tiles_ref[...] = total.astype(jnp.bfloat16)

    for c in range(CHUNKS):
        pl.when(me != c)(
            remote(tap_all.at[c], tap_all.at[c], all_s.at[c], all_r.at[c], c).wait_recv
        )
    for c in range(CHUNKS):
        taps_ref[:, c * LANES : (c + 1) * LANES] = tap_all[c, 0:KERNEL, :]

    finish_exchange(tile_copies)
    finish_all_to_all(heads_out, heads_in, heads_s, heads_r)
    finish_all_to_all(grads_out, grads_in, grads_s, grads_r)
    finish_exchange(back_copies)
    for c in range(CHUNKS):
        pl.when(me != c)(tap_copies[c].wait_send)

    @pl.when(me < CHUNKS)
    def _():
        @pl.loop(1, n)
        def _(step):
            peer = lax.rem(me + step, n)
            remote(tap_all.at[me], tap_all.at[me], all_s.at[peer], all_r.at[me], peer).wait_send()


def per_device_heads(n, tile_embed, grad_output, query_key_value_weight, conv_weight, neighbours):
    bf16, f32, i32 = jnp.bfloat16, jnp.float32, jnp.int32
    taps = KERNEL * ROWS
    dma = pltpu.SemaphoreType.DMA
    vmem = pl.BlockSpec(memory_space=pltpu.VMEM)
    return pl.pallas_call(
        functools.partial(slide_kernel, n),
        out_shape=(
            jax.ShapeDtypeStruct((ROWS, MODEL_WIDTH), bf16),
            jax.ShapeDtypeStruct((ROWS, MODEL_WIDTH), bf16),
            jax.ShapeDtypeStruct((KERNEL, MODEL_WIDTH), f32),
        ),
        in_specs=[vmem, vmem, pl.BlockSpec(memory_space=pl.ANY), vmem, vmem],
        out_specs=(vmem, vmem, vmem),
        scratch_shapes=[
            pltpu.VMEM(query_key_value_weight.shape, bf16),
            pltpu.VMEM((LANES, ROWS), i32),
            pltpu.VMEM((ROWS, LANES), i32),
            pltpu.VMEM((ROWS, LANES), i32),
            pltpu.VMEM((2 * ROWS, MODEL_WIDTH), bf16),
            pltpu.VMEM((taps, MODEL_WIDTH), f32),
            pltpu.VMEM((taps, MODEL_WIDTH), bf16),
            pltpu.VMEM((taps, ROWS), bf16),
            pltpu.VMEM((taps, 2 * ROWS), bf16),
            pltpu.VMEM((taps, 2 * ROWS), bf16),
            pltpu.VMEM((taps, 2 * ROWS), bf16),
            pltpu.VMEM((ROWS, MODEL_WIDTH), bf16),
            pltpu.VMEM((n, PACKED, LANES), bf16),
            pltpu.VMEM((n, PACKED, LANES), bf16),
            pltpu.VMEM((n, PACKED, LANES), bf16),
            pltpu.VMEM((n, PACKED, LANES), bf16),
            pltpu.VMEM((2 * ROWS, MODEL_WIDTH), bf16),
            pltpu.VMEM((2 * ROWS, MODEL_WIDTH), bf16),
            pltpu.VMEM((CHUNKS, 16, LANES), f32),
            pltpu.VMEM((n, 16, LANES), f32),
            pltpu.VMEM((CHUNKS, 16, LANES), f32),
            dma,
            dma((2,)),
            dma((2,)),
            dma((n,)),
            dma((n,)),
            dma((n,)),
            dma((n,)),
            dma((2,)),
            dma((2,)),
            dma((CHUNKS,)),
            dma((n,)),
            dma((n,)),
            dma((CHUNKS,)),
        ],
        compiler_params=pltpu.CompilerParams(
            collective_id=0, has_side_effects=True, vmem_limit_bytes=VMEM_BYTES
        ),
    )(tile_embed, grad_output, query_key_value_weight, conv_weight, neighbours)


def per_device_choice(n, tile_embed, *rest):
    if n == HEAD_COUNT and tile_embed.shape[0] == ROWS:
        return per_device_heads(n, tile_embed, *rest)
    return per_device(tile_embed, *rest)


def solution(mesh):
    placed = (
        P(("slide", "seq"), None),
        P(("slide", "seq"), None),
        P(),
        P(),
        P(None, ("slide", "seq")),
    )
    return jax.shard_map(
        functools.partial(per_device_choice, mesh.shape["seq"]),
        mesh=mesh,
        in_specs=placed,
        out_specs=(P(("slide", "seq"), None), P(("slide", "seq"), None), P("slide", None)),
        check_vma=False,
    )
```

```python
import functools

import jax
import jax.numpy as jnp
from jax import lax
from jax.experimental import pallas as pl
from jax.experimental.pallas import tpu as pltpu
from jax.sharding import PartitionSpec as P

MODEL_WIDTH = 768
HEAD_COUNT = 16
HEAD_SIZE = 48
DILATION_STEP = 4
KERNEL = 9
REACH = 127


def extended_2(shard, sides, width):
    for axis, dim in sides:
        count, length = (lax.axis_size(axis), shard.shape[dim])
        up = [(i, (i + 1) % count) for i in range(count - 1)]
        down = [(j, i) for i, j in up]
        last = lax.slice_in_dim(shard, length - width, length, axis=dim)
        leading = lax.slice_in_dim(shard, 0, width, axis=dim)
        before = lax.ppermute(last, axis, up)
        after = lax.ppermute(leading, axis, down)
        shard = jnp.concatenate([before, shard, after], axis=dim)
    return shard


def from_behind(value, axis, steps):
    count = lax.axis_size(axis)
    leading, last = (max(0, -steps), min(count, count - steps))
    return lax.ppermute(value, axis, [(source, source + steps) for source in range(leading, last)])


def select_dilated(full_result, item_count):
    each_group = HEAD_COUNT // DILATION_STEP
    five_value = full_result.reshape(
        item_count // DILATION_STEP, DILATION_STEP, each_group, DILATION_STEP, HEAD_SIZE
    )
    return jnp.stack(
        [
            five_value[:, residue_index, :, residue_index, :]
            for residue_index in range(DILATION_STEP)
        ],
        axis=2,
    ).reshape(item_count // DILATION_STEP, MODEL_WIDTH)


def spread_dilated(selected_rows):
    item_count = selected_rows.shape[0]
    five_value = selected_rows.reshape(
        item_count, 1, HEAD_COUNT // DILATION_STEP, DILATION_STEP, HEAD_SIZE
    )
    unit_vector = jnp.eye(DILATION_STEP, dtype=selected_rows.dtype).reshape(
        1, DILATION_STEP, 1, DILATION_STEP, 1
    )
    return (five_value * unit_vector).reshape(item_count * DILATION_STEP, MODEL_WIDTH)


def contract_last(left, right):
    return lax.dot_general(
        left, right, (((1,), (1,)), ((), ())), preferred_element_type=jnp.float32
    )


def contract_first(left, right):
    return lax.dot_general(
        left, right, (((0,), (0,)), ((), ())), preferred_element_type=jnp.float32
    )


def head_forward(items):
    queries, keys, values, douts = items
    scale = HEAD_SIZE ** (-0.5)
    scores = contract_last(queries, keys) * scale
    top = jnp.max(scores, axis=1, keepdims=True)
    log_total = top + jnp.log(jnp.sum(jnp.exp(scores - top), axis=1, keepdims=True))
    weights = jnp.exp(scores - log_total)
    weights_low = weights.astype(jnp.bfloat16)
    output = jnp.dot(weights_low, values, preferred_element_type=jnp.float32).astype(jnp.bfloat16)
    delta = jnp.sum(douts.astype(jnp.float32) * output.astype(jnp.float32), axis=1)
    dprob = contract_last(douts, values)
    dscore = (weights * (dprob - delta[:, None]) * scale).astype(jnp.bfloat16)
    grad_q = jnp.dot(dscore, keys, preferred_element_type=jnp.float32).astype(jnp.bfloat16)
    return (output, log_total[:, 0], delta, grad_q)


def head_keyside(items):
    query_piece, dout_piece, lse_piece, delta_piece, local_keys, local_values = items
    scale = HEAD_SIZE ** (-0.5)
    piece_scores = contract_last(query_piece, local_keys) * scale
    piece_weights = jnp.exp(piece_scores - lse_piece[:, None])
    value_part = contract_first(piece_weights.astype(jnp.bfloat16), dout_piece)
    piece_dprob = contract_last(dout_piece, local_values)
    piece_dscore = (piece_weights * (piece_dprob - delta_piece[:, None]) * scale).astype(
        jnp.bfloat16
    )
    key_part = contract_first(piece_dscore, query_piece)
    return (key_part, value_part)


def heads_lead(values, item_count):
    return jnp.transpose(values.reshape(item_count, HEAD_COUNT, HEAD_SIZE), (1, 0, 2))


def per_device(tile_embed, grad_output, query_key_value_weight, conv_weight, neighbours):
    count_of_rows = tile_embed.shape[0]
    partial_rows = count_of_rows // DILATION_STEP
    each_group = HEAD_COUNT // DILATION_STEP
    extended = extended_2(tile_embed, (("seq", 0),), REACH)
    valid = neighbours >= 0
    offset = lax.axis_index("seq") * count_of_rows - REACH
    local_index = jnp.where(valid, neighbours - offset, 0)
    valid_mask = valid.astype(jnp.float32)
    near_rows = [
        extended[local_index[k]].astype(jnp.float32) * valid_mask[k][:, None] for k in range(KERNEL)
    ]
    summed = tile_embed.astype(jnp.float32)
    for k in range(KERNEL):
        summed = summed + conv_weight[k][None, :] * near_rows[k]
    mixed_tiles = summed.astype(jnp.bfloat16)
    split_weights = query_key_value_weight.reshape(
        MODEL_WIDTH, 3, each_group, DILATION_STEP, HEAD_SIZE
    )
    per_residue_class = mixed_tiles.reshape(partial_rows, DILATION_STEP, MODEL_WIDTH)
    residue_weights = [
        split_weights[:, :, :, residue_index, :].reshape(MODEL_WIDTH, 3 * each_group * HEAD_SIZE)
        for residue_index in range(DILATION_STEP)
    ]
    projected = jnp.stack(
        [
            jnp.dot(
                per_residue_class[:, residue_index, :],
                residue_weights[residue_index],
                preferred_element_type=jnp.float32,
            )
            .astype(jnp.bfloat16)
            .reshape(partial_rows, 3, each_group, HEAD_SIZE)
            for residue_index in range(DILATION_STEP)
        ],
        axis=3,
    )
    query_sel = projected[:, 0].reshape(partial_rows, MODEL_WIDTH)
    key_sel = projected[:, 1].reshape(partial_rows, MODEL_WIDTH)
    value_sel = projected[:, 2].reshape(partial_rows, MODEL_WIDTH)
    dout_sel = select_dilated(grad_output, count_of_rows)
    key_all, value_all = (
        lax.all_gather(key_sel, "seq", axis=0, tiled=True),
        lax.all_gather(value_sel, "seq", axis=0, tiled=True),
    )
    total_keys = key_all.shape[0]
    output_h, lse_h, delta_h, grad_q_h = lax.map(
        head_forward,
        (
            heads_lead(query_sel, partial_rows),
            heads_lead(key_all, total_keys),
            heads_lead(value_all, total_keys),
            heads_lead(dout_sel, partial_rows),
        ),
    )
    grad_q = jnp.transpose(grad_q_h, (1, 0, 2)).reshape(partial_rows, MODEL_WIDTH)
    output_sel = jnp.transpose(output_h, (1, 0, 2)).reshape(partial_rows, MODEL_WIDTH)
    lse_all, delta_all = (
        lax.all_gather(lse_h.T, "seq", axis=0, tiled=True),
        lax.all_gather(delta_h.T, "seq", axis=0, tiled=True),
    )
    local_keys_h = heads_lead(key_sel, partial_rows)
    local_values_h = heads_lead(value_sel, partial_rows)
    query_piece = lax.all_gather(query_sel, "seq", axis=0, tiled=True)
    dout_piece = lax.all_gather(dout_sel, "seq", axis=0, tiled=True)
    item_count = query_piece.shape[0]
    key_part, value_part = lax.map(
        head_keyside,
        (
            heads_lead(query_piece, item_count),
            heads_lead(dout_piece, item_count),
            lse_all.T,
            delta_all.T,
            local_keys_h,
            local_values_h,
        ),
    )
    grad_k = (
        jnp.transpose(key_part, (1, 0, 2)).reshape(partial_rows, MODEL_WIDTH).astype(jnp.bfloat16)
    )
    grad_v = (
        jnp.transpose(value_part, (1, 0, 2)).reshape(partial_rows, MODEL_WIDTH).astype(jnp.bfloat16)
    )
    attended = spread_dilated(output_sel)
    gradient_list = (grad_q, grad_k, grad_v)
    dmixed_parts = []
    for residue_index in range(DILATION_STEP):
        stacked = jnp.stack(
            [
                group_index.reshape(partial_rows, each_group, DILATION_STEP, HEAD_SIZE)[
                    :, :, residue_index, :
                ]
                for group_index in gradient_list
            ],
            axis=1,
        )
        dmixed_parts.append(
            contract_last(
                stacked.reshape(partial_rows, 3 * each_group * HEAD_SIZE),
                residue_weights[residue_index],
            )
        )
    dmixed = jnp.stack(dmixed_parts, axis=1).reshape(count_of_rows, MODEL_WIDTH)
    conv_terms = jnp.stack([jnp.sum(dmixed * near_rows[k], axis=0) for k in range(KERNEL)])
    grad_conv = lax.psum(conv_terms, "seq")
    contrib = jnp.zeros((count_of_rows + 2 * REACH, MODEL_WIDTH), jnp.float32)
    for k in range(KERNEL):
        contrib = contrib.at[local_index[k]].add(
            conv_weight[k][None, :] * dmixed * valid_mask[k][:, None]
        )
    from_above = from_behind(contrib[:REACH], "seq", -1)
    from_below = from_behind(
        contrib[REACH + count_of_rows :].astype(jnp.bfloat16), "seq", 1
    ).astype(jnp.float32)
    total = dmixed + contrib[REACH : REACH + count_of_rows]
    total = total + jnp.pad(from_below, ((0, count_of_rows - REACH), (0, 0)))
    total = total + jnp.pad(from_above, ((count_of_rows - REACH, 0), (0, 0)))
    grad_tiles = total.astype(jnp.bfloat16)
    return (attended, grad_tiles, grad_conv)


ROWS = 128
PART = ROWS // DILATION_STEP
PACKED = 48
LANES = 128
CHUNKS = MODEL_WIDTH // LANES
VMEM_BYTES = 56 * 1024 * 1024


def bf16_dot(left, right):
    return jnp.dot(left, right, preferred_element_type=jnp.float32)


def one_hot(column, positions):
    return jnp.where(column == positions, 1.0, 0.0).astype(jnp.bfloat16)


def remote(source, target, send_sem, recv_sem, peer):
    return pltpu.make_async_remote_copy(
        src_ref=source,
        dst_ref=target,
        send_sem=send_sem,
        recv_sem=recv_sem,
        device_id={"seq": peer},
        device_id_type=pl.DeviceIdType.MESH,
    )


def slide_kernel(
    n,
    tile_ref,
    dout_ref,
    weight_hbm,
    conv_ref,
    near_ref,
    attended_ref,
    tiles_ref,
    taps_ref,
    weight,
    near_pad,
    columns,
    columns_perm,
    halo,
    gathered_own,
    gathered,
    hot_own,
    hot_halo,
    back_own,
    back_halo,
    dout_perm,
    heads_out,
    heads_in,
    grads_out,
    grads_in,
    split,
    back_rows,
    tap_part,
    tap_in,
    tap_all,
    weight_sem,
    halo_s,
    halo_r,
    heads_s,
    heads_r,
    grads_s,
    grads_r,
    back_s,
    back_r,
    tap_s,
    tap_r,
    all_s,
    all_r,
):
    me = lax.axis_index("seq")
    load_weight = pltpu.make_async_copy(weight_hbm, weight, weight_sem)
    load_weight.start()

    barrier = pltpu.get_barrier_semaphore()

    @pl.loop(1, n)
    def _(step):
        pl.semaphore_signal(
            barrier,
            inc=1,
            device_id={"seq": lax.rem(me + step, n)},
            device_id_type=pl.DeviceIdType.MESH,
        )

    near = near_ref[...]
    near_pad[...] = jnp.full((LANES, ROWS), -1, jnp.int32)
    near_pad[0:KERNEL, :] = jnp.where(near >= 0, near - (me - 1) * ROWS, -1)
    columns[...] = near_pad[...].T
    for r in range(DILATION_STEP):
        columns_perm[r * PART : (r + 1) * PART, :] = columns[pl.ds(r, PART, stride=DILATION_STEP), :]
    lane = lax.broadcasted_iota(jnp.int32, (ROWS, ROWS), 1)
    row = lax.broadcasted_iota(jnp.int32, (ROWS, ROWS), 0)
    tile_of_lane = (lane % PART) * DILATION_STEP + lane // PART
    tile_of_row = (row % PART) * DILATION_STEP + row // PART
    for k in range(KERNEL):
        column = columns_perm[:, k : k + 1]
        rows = slice(k * ROWS, (k + 1) * ROWS)
        hot_own[rows, :] = one_hot(column, lane + ROWS)
        hot_halo[rows, 0:ROWS] = one_hot(column, lane)
        hot_halo[rows, ROWS : 2 * ROWS] = one_hot(column, lane + 2 * ROWS)
    to_perm = one_hot(tile_of_row, lane)
    dout_perm[...] = bf16_dot(to_perm, dout_ref[...]).astype(jnp.bfloat16)

    pl.semaphore_wait(barrier, n - 1)

    def exchange(source, target, send_sem, recv_sem):
        up = remote(source, target.at[pl.ds(0, ROWS)], send_sem.at[0], recv_sem.at[0], me + 1)
        down = remote(source, target.at[pl.ds(ROWS, ROWS)], send_sem.at[1], recv_sem.at[1], me - 1)
        return up, down

    def start_exchange(copies):
        pl.when(me < n - 1)(copies[0].start)
        pl.when(me > 0)(copies[1].start)

    def arrive_exchange(copies):
        pl.when(me > 0)(copies[0].wait_recv)
        pl.when(me < n - 1)(copies[1].wait_recv)

    def finish_exchange(copies):
        pl.when(me < n - 1)(copies[0].wait_send)
        pl.when(me > 0)(copies[1].wait_send)

    def clear_ends(target):
        @pl.when(me == 0)
        def _():
            target[0:ROWS, :] = jnp.zeros((ROWS, MODEL_WIDTH), jnp.bfloat16)

        @pl.when(me == n - 1)
        def _():
            target[ROWS : 2 * ROWS, :] = jnp.zeros((ROWS, MODEL_WIDTH), jnp.bfloat16)

    tile_copies = exchange(tile_ref, halo, halo_s, halo_r)
    start_exchange(tile_copies)
    clear_ends(halo)
    clear_ends(back_rows)
    gathered_own[...] = bf16_dot(hot_own[...], tile_ref[...])
    for h in range(HEAD_COUNT):
        r = h % DILATION_STEP
        piece = dout_perm[r * PART : (r + 1) * PART, h * HEAD_SIZE : (h + 1) * HEAD_SIZE]
        heads_out[h, PART:PACKED, 32:80] = piece[0:16]
        heads_out[h, PART:PACKED, 80:128] = piece[16:32]
    for k in range(KERNEL):
        column = columns[:, k : k + 1]
        rows = slice(k * ROWS, (k + 1) * ROWS)
        own = one_hot(column, tile_of_lane + ROWS)
        back_own[rows, 0:ROWS] = own
        back_own[rows, ROWS : 2 * ROWS] = own
        back_halo[rows, 0:ROWS] = one_hot(column, tile_of_lane)
        back_halo[rows, ROWS : 2 * ROWS] = one_hot(column, tile_of_lane + 2 * ROWS)

    arrive_exchange(tile_copies)
    gathered[...] = (gathered_own[...] + bf16_dot(hot_halo[...], halo[...])).astype(jnp.bfloat16)

    def tap_rows(k):
        return gathered[k * ROWS : (k + 1) * ROWS, :].astype(jnp.float32)

    summed = tap_rows(KERNEL // 2)
    for k in range(KERNEL):
        summed = summed + conv_ref[k : k + 1, :] * tap_rows(k)
    mixed = summed.astype(jnp.bfloat16)

    load_weight.wait()
    projected = [
        bf16_dot(mixed, weight[:, s * MODEL_WIDTH : (s + 1) * MODEL_WIDTH]).astype(jnp.bfloat16)
        for s in range(3)
    ]
    for h in range(HEAD_COUNT):
        r = h % DILATION_STEP
        q, k, v = [
            x[r * PART : (r + 1) * PART, h * HEAD_SIZE : (h + 1) * HEAD_SIZE] for x in projected
        ]
        heads_out[h, 0:PART, :] = jnp.concatenate([q, k, v[:, 0:32]], axis=1)
        heads_out[h, PART:PACKED, 0:16] = v[0:16, 32:48]
        heads_out[h, PART:PACKED, 16:32] = v[16:32, 32:48]

    def all_to_all(source, target, send_sem, recv_sem):
        @pl.loop(1, n)
        def _(step):
            peer = me ^ (n - step)
            remote(
                source.at[peer], target.at[me], send_sem.at[peer], recv_sem.at[me], peer
            ).start()

        target[me] = source[me]

        @pl.loop(1, n)
        def _(step):
            peer = lax.rem(me + n - step, n)
            remote(
                source.at[peer], target.at[peer], send_sem.at[peer], recv_sem.at[peer], peer
            ).wait_recv()

    def finish_all_to_all(source, target, send_sem, recv_sem):
        @pl.loop(1, n)
        def _(step):
            peer = lax.rem(me + step, n)
            remote(
                source.at[peer], target.at[me], send_sem.at[peer], recv_sem.at[me], peer
            ).wait_send()

    all_to_all(heads_out, heads_in, heads_s, heads_r)

    keys_total = n * PART
    front = heads_in[:, 0:PART, :].reshape(keys_total, LANES)
    rest = heads_in[:, PART:PACKED, :]
    q = front[:, 0:48]
    k = front[:, 48:96]
    v_tail = jnp.concatenate([rest[:, :, 0:16], rest[:, :, 16:32]], axis=1).reshape(keys_total, 16)
    v = jnp.concatenate([front[:, 96:128], v_tail], axis=1)
    do = jnp.concatenate([rest[:, :, 32:80], rest[:, :, 80:128]], axis=1).reshape(keys_total, 48)
    scale = HEAD_SIZE ** (-0.5)
    scores = contract_last(k, q) * scale
    top = jnp.max(scores, axis=0, keepdims=True)
    grown = jnp.exp(scores - top)
    prob = grown * (1.0 / jnp.sum(grown, axis=0, keepdims=True))
    prob_low = prob.astype(jnp.bfloat16)
    out_t = bf16_dot(v.T, prob_low).astype(jnp.bfloat16)
    delta = jnp.sum(
        do.T.astype(jnp.float32) * out_t.astype(jnp.float32), axis=0, keepdims=True
    )
    dprob = contract_last(v, do)
    dscore = (prob * (dprob - delta) * scale).astype(jnp.bfloat16)
    out = out_t.T
    dq = bf16_dot(k.T, dscore).astype(jnp.bfloat16).T
    dk = bf16_dot(dscore, q).astype(jnp.bfloat16)
    dv = bf16_dot(prob_low, do).astype(jnp.bfloat16)
    grads_out[:, 0:PART, :] = jnp.concatenate([out, dq, dk[:, 0:32]], axis=1).reshape(
        n, PART, LANES
    )
    dk_tail = dk[:, 32:48].reshape(n, PART, 16)
    dv_rows = dv.reshape(n, PART, HEAD_SIZE)
    grads_out[:, PART:PACKED, :] = jnp.concatenate(
        [dk_tail[:, 0:16], dk_tail[:, 16:32], dv_rows[:, 0:16], dv_rows[:, 16:32]], axis=2
    )
    all_to_all(grads_out, grads_in, grads_s, grads_r)

    blank = jnp.zeros((PART, HEAD_SIZE), jnp.bfloat16)
    grown_rows = [[], [], [], []]
    for r in range(DILATION_STEP):
        lists = [[], [], [], []]
        for h in range(HEAD_COUNT):
            if h % DILATION_STEP != r:
                for entry in lists:
                    entry.append(blank)
                continue
            x = grads_in[h, 0:PART, :]
            y = grads_in[h, PART:PACKED, :]
            lists[0].append(x[:, 0:48])
            lists[1].append(x[:, 48:96])
            tail = jnp.concatenate([y[:, 0:16], y[:, 16:32]], axis=0)
            lists[2].append(jnp.concatenate([x[:, 96:128], tail], axis=1))
            lists[3].append(jnp.concatenate([y[:, 32:80], y[:, 80:128]], axis=0))
        for s in range(4):
            grown_rows[s].append(jnp.concatenate(lists[s], axis=1))
    out_perm, dq_perm, dk_perm, dv_perm = [jnp.concatenate(x, axis=0) for x in grown_rows]
    dmixed = jnp.zeros((ROWS, MODEL_WIDTH), jnp.float32)
    for s, part in enumerate((dq_perm, dk_perm, dv_perm)):
        dmixed = dmixed + contract_last(part, weight[:, s * MODEL_WIDTH : (s + 1) * MODEL_WIDTH])
    high = dmixed.astype(jnp.bfloat16)
    split[0:ROWS, :] = high
    split[ROWS : 2 * ROWS, :] = (dmixed - high.astype(jnp.float32)).astype(jnp.bfloat16)
    back_copies = exchange(split.at[pl.ds(0, ROWS)], back_rows, back_s, back_r)

    tap_part[...] = jnp.zeros_like(tap_part)
    for k in range(KERNEL):
        term = jnp.sum(dmixed * tap_rows(k), axis=0, keepdims=True)
        for c in range(CHUNKS):
            tap_part[c, k : k + 1, :] = term[:, c * LANES : (c + 1) * LANES]
    tap_copies = [
        remote(tap_part.at[c], tap_in.at[me], tap_s.at[c], tap_r.at[me], c) for c in range(CHUNKS)
    ]
    for c in range(CHUNKS):
        pl.when(me != c)(tap_copies[c].start)
    start_exchange(back_copies)

    natural = one_hot(row, tile_of_lane)
    attended_ref[...] = bf16_dot(natural, out_perm).astype(jnp.bfloat16)
    own_back = bf16_dot(back_own[...], split[...])
    total = own_back[(KERNEL // 2) * ROWS : (KERNEL // 2 + 1) * ROWS]
    for k in range(KERNEL):
        j = KERNEL - 1 - k
        total = total + conv_ref[k : k + 1, :] * own_back[j * ROWS : (j + 1) * ROWS]

    @pl.when(me < CHUNKS)
    def _():
        tap_in[me] = tap_part[me]

        @pl.loop(1, n)
        def _(step):
            peer = lax.rem(me + n - step, n)
            remote(tap_part.at[0], tap_in.at[peer], tap_s.at[0], tap_r.at[peer], peer).wait_recv()

        tap_all[me] = jnp.sum(tap_in[...], axis=0)

        @pl.loop(1, n)
        def _(step):
            peer = lax.rem(me + step, n)
            remote(tap_all.at[me], tap_all.at[me], all_s.at[peer], all_r.at[me], peer).start()

    arrive_exchange(back_copies)
    halo_back = bf16_dot(back_halo[...], back_rows[...])
    for k in range(KERNEL):
        j = KERNEL - 1 - k
        total = total + conv_ref[k : k + 1, :] * halo_back[j * ROWS : (j + 1) * ROWS]
    tiles_ref[...] = total.astype(jnp.bfloat16)

    for c in range(CHUNKS):
        pl.when(me != c)(
            remote(tap_all.at[c], tap_all.at[c], all_s.at[c], all_r.at[c], c).wait_recv
        )
    for c in range(CHUNKS):
        taps_ref[:, c * LANES : (c + 1) * LANES] = tap_all[c, 0:KERNEL, :]

    finish_exchange(tile_copies)
    finish_all_to_all(heads_out, heads_in, heads_s, heads_r)
    finish_all_to_all(grads_out, grads_in, grads_s, grads_r)
    finish_exchange(back_copies)
    for c in range(CHUNKS):
        pl.when(me != c)(tap_copies[c].wait_send)

    @pl.when(me < CHUNKS)
    def _():
        @pl.loop(1, n)
        def _(step):
            peer = lax.rem(me + step, n)
            remote(tap_all.at[me], tap_all.at[me], all_s.at[peer], all_r.at[me], peer).wait_send()


def per_device_heads(n, tile_embed, grad_output, query_key_value_weight, conv_weight, neighbours):
    bf16, f32, i32 = jnp.bfloat16, jnp.float32, jnp.int32
    taps = KERNEL * ROWS
    dma = pltpu.SemaphoreType.DMA
    vmem = pl.BlockSpec(memory_space=pltpu.VMEM)
    return pl.pallas_call(
        functools.partial(slide_kernel, n),
        out_shape=(
            jax.ShapeDtypeStruct((ROWS, MODEL_WIDTH), bf16),
            jax.ShapeDtypeStruct((ROWS, MODEL_WIDTH), bf16),
            jax.ShapeDtypeStruct((KERNEL, MODEL_WIDTH), f32),
        ),
        in_specs=[vmem, vmem, pl.BlockSpec(memory_space=pl.ANY), vmem, vmem],
        out_specs=(vmem, vmem, vmem),
        scratch_shapes=[
            pltpu.VMEM(query_key_value_weight.shape, bf16),
            pltpu.VMEM((LANES, ROWS), i32),
            pltpu.VMEM((ROWS, LANES), i32),
            pltpu.VMEM((ROWS, LANES), i32),
            pltpu.VMEM((2 * ROWS, MODEL_WIDTH), bf16),
            pltpu.VMEM((taps, MODEL_WIDTH), f32),
            pltpu.VMEM((taps, MODEL_WIDTH), bf16),
            pltpu.VMEM((taps, ROWS), bf16),
            pltpu.VMEM((taps, 2 * ROWS), bf16),
            pltpu.VMEM((taps, 2 * ROWS), bf16),
            pltpu.VMEM((taps, 2 * ROWS), bf16),
            pltpu.VMEM((ROWS, MODEL_WIDTH), bf16),
            pltpu.VMEM((n, PACKED, LANES), bf16),
            pltpu.VMEM((n, PACKED, LANES), bf16),
            pltpu.VMEM((n, PACKED, LANES), bf16),
            pltpu.VMEM((n, PACKED, LANES), bf16),
            pltpu.VMEM((2 * ROWS, MODEL_WIDTH), bf16),
            pltpu.VMEM((2 * ROWS, MODEL_WIDTH), bf16),
            pltpu.VMEM((CHUNKS, 16, LANES), f32),
            pltpu.VMEM((n, 16, LANES), f32),
            pltpu.VMEM((CHUNKS, 16, LANES), f32),
            dma,
            dma((2,)),
            dma((2,)),
            dma((n,)),
            dma((n,)),
            dma((n,)),
            dma((n,)),
            dma((2,)),
            dma((2,)),
            dma((CHUNKS,)),
            dma((n,)),
            dma((n,)),
            dma((CHUNKS,)),
        ],
        compiler_params=pltpu.CompilerParams(
            collective_id=0, has_side_effects=True, vmem_limit_bytes=VMEM_BYTES
        ),
    )(tile_embed, grad_output, query_key_value_weight, conv_weight, neighbours)


def hand_on_kernel(a_ref, b_ref, c_ref, a_out, b_out, c_out):
    a_out[...] = a_ref[...]
    b_out[...] = b_ref[...]
    c_out[...] = c_ref[...]


def hand_on(*arrays):
    vmem = pl.BlockSpec(memory_space=pltpu.VMEM)
    return pl.pallas_call(
        hand_on_kernel,
        out_shape=tuple(jax.ShapeDtypeStruct(x.shape, x.dtype) for x in arrays),
        in_specs=[vmem] * 3,
        out_specs=(vmem,) * 3,
    )(*arrays)


def per_device_choice(n, tile_embed, *rest):
    if n == HEAD_COUNT and tile_embed.shape[0] == ROWS:
        return hand_on(*per_device_heads(n, tile_embed, *rest))
    return per_device(tile_embed, *rest)


def solution(mesh):
    placed = (
        P(("slide", "seq"), None),
        P(("slide", "seq"), None),
        P(),
        P(),
        P(None, ("slide", "seq")),
    )
    return jax.shard_map(
        functools.partial(per_device_choice, mesh.shape["seq"]),
        mesh=mesh,
        in_specs=placed,
        out_specs=(P(("slide", "seq"), None), P(("slide", "seq"), None), P("slide", None)),
        check_vma=False,
    )
```

```python
import functools

import jax
import jax.numpy as jnp
from jax import lax
from jax.experimental import pallas as pl
from jax.experimental.pallas import tpu as pltpu
from jax.sharding import PartitionSpec as P

MODEL_WIDTH = 768
HEAD_COUNT = 16
HEAD_SIZE = 48
DILATION_STEP = 4
KERNEL = 9
REACH = 127


def extended_2(shard, sides, width):
    for axis, dim in sides:
        count, length = (lax.axis_size(axis), shard.shape[dim])
        up = [(i, (i + 1) % count) for i in range(count - 1)]
        down = [(j, i) for i, j in up]
        last = lax.slice_in_dim(shard, length - width, length, axis=dim)
        leading = lax.slice_in_dim(shard, 0, width, axis=dim)
        before = lax.ppermute(last, axis, up)
        after = lax.ppermute(leading, axis, down)
        shard = jnp.concatenate([before, shard, after], axis=dim)
    return shard


def from_behind(value, axis, steps):
    count = lax.axis_size(axis)
    leading, last = (max(0, -steps), min(count, count - steps))
    return lax.ppermute(value, axis, [(source, source + steps) for source in range(leading, last)])


def select_dilated(full_result, item_count):
    each_group = HEAD_COUNT // DILATION_STEP
    five_value = full_result.reshape(
        item_count // DILATION_STEP, DILATION_STEP, each_group, DILATION_STEP, HEAD_SIZE
    )
    return jnp.stack(
        [
            five_value[:, residue_index, :, residue_index, :]
            for residue_index in range(DILATION_STEP)
        ],
        axis=2,
    ).reshape(item_count // DILATION_STEP, MODEL_WIDTH)


def spread_dilated(selected_rows):
    item_count = selected_rows.shape[0]
    five_value = selected_rows.reshape(
        item_count, 1, HEAD_COUNT // DILATION_STEP, DILATION_STEP, HEAD_SIZE
    )
    unit_vector = jnp.eye(DILATION_STEP, dtype=selected_rows.dtype).reshape(
        1, DILATION_STEP, 1, DILATION_STEP, 1
    )
    return (five_value * unit_vector).reshape(item_count * DILATION_STEP, MODEL_WIDTH)


def contract_last(left, right):
    return lax.dot_general(
        left, right, (((1,), (1,)), ((), ())), preferred_element_type=jnp.float32
    )


def contract_first(left, right):
    return lax.dot_general(
        left, right, (((0,), (0,)), ((), ())), preferred_element_type=jnp.float32
    )


def head_forward(items):
    queries, keys, values, douts = items
    scale = HEAD_SIZE ** (-0.5)
    scores = contract_last(queries, keys) * scale
    top = jnp.max(scores, axis=1, keepdims=True)
    log_total = top + jnp.log(jnp.sum(jnp.exp(scores - top), axis=1, keepdims=True))
    weights = jnp.exp(scores - log_total)
    weights_low = weights.astype(jnp.bfloat16)
    output = jnp.dot(weights_low, values, preferred_element_type=jnp.float32).astype(jnp.bfloat16)
    delta = jnp.sum(douts.astype(jnp.float32) * output.astype(jnp.float32), axis=1)
    dprob = contract_last(douts, values)
    dscore = (weights * (dprob - delta[:, None]) * scale).astype(jnp.bfloat16)
    grad_q = jnp.dot(dscore, keys, preferred_element_type=jnp.float32).astype(jnp.bfloat16)
    return (output, log_total[:, 0], delta, grad_q)


def head_keyside(items):
    query_piece, dout_piece, lse_piece, delta_piece, local_keys, local_values = items
    scale = HEAD_SIZE ** (-0.5)
    piece_scores = contract_last(query_piece, local_keys) * scale
    piece_weights = jnp.exp(piece_scores - lse_piece[:, None])
    value_part = contract_first(piece_weights.astype(jnp.bfloat16), dout_piece)
    piece_dprob = contract_last(dout_piece, local_values)
    piece_dscore = (piece_weights * (piece_dprob - delta_piece[:, None]) * scale).astype(
        jnp.bfloat16
    )
    key_part = contract_first(piece_dscore, query_piece)
    return (key_part, value_part)


def heads_lead(values, item_count):
    return jnp.transpose(values.reshape(item_count, HEAD_COUNT, HEAD_SIZE), (1, 0, 2))


def per_device(tile_embed, grad_output, query_key_value_weight, conv_weight, neighbours):
    count_of_rows = tile_embed.shape[0]
    partial_rows = count_of_rows // DILATION_STEP
    each_group = HEAD_COUNT // DILATION_STEP
    extended = extended_2(tile_embed, (("seq", 0),), REACH)
    valid = neighbours >= 0
    offset = lax.axis_index("seq") * count_of_rows - REACH
    local_index = jnp.where(valid, neighbours - offset, 0)
    valid_mask = valid.astype(jnp.float32)
    near_rows = [
        extended[local_index[k]].astype(jnp.float32) * valid_mask[k][:, None] for k in range(KERNEL)
    ]
    summed = tile_embed.astype(jnp.float32)
    for k in range(KERNEL):
        summed = summed + conv_weight[k][None, :] * near_rows[k]
    mixed_tiles = summed.astype(jnp.bfloat16)
    split_weights = query_key_value_weight.reshape(
        MODEL_WIDTH, 3, each_group, DILATION_STEP, HEAD_SIZE
    )
    per_residue_class = mixed_tiles.reshape(partial_rows, DILATION_STEP, MODEL_WIDTH)
    residue_weights = [
        split_weights[:, :, :, residue_index, :].reshape(MODEL_WIDTH, 3 * each_group * HEAD_SIZE)
        for residue_index in range(DILATION_STEP)
    ]
    projected = jnp.stack(
        [
            jnp.dot(
                per_residue_class[:, residue_index, :],
                residue_weights[residue_index],
                preferred_element_type=jnp.float32,
            )
            .astype(jnp.bfloat16)
            .reshape(partial_rows, 3, each_group, HEAD_SIZE)
            for residue_index in range(DILATION_STEP)
        ],
        axis=3,
    )
    query_sel = projected[:, 0].reshape(partial_rows, MODEL_WIDTH)
    key_sel = projected[:, 1].reshape(partial_rows, MODEL_WIDTH)
    value_sel = projected[:, 2].reshape(partial_rows, MODEL_WIDTH)
    dout_sel = select_dilated(grad_output, count_of_rows)
    key_all, value_all = (
        lax.all_gather(key_sel, "seq", axis=0, tiled=True),
        lax.all_gather(value_sel, "seq", axis=0, tiled=True),
    )
    total_keys = key_all.shape[0]
    output_h, lse_h, delta_h, grad_q_h = lax.map(
        head_forward,
        (
            heads_lead(query_sel, partial_rows),
            heads_lead(key_all, total_keys),
            heads_lead(value_all, total_keys),
            heads_lead(dout_sel, partial_rows),
        ),
    )
    grad_q = jnp.transpose(grad_q_h, (1, 0, 2)).reshape(partial_rows, MODEL_WIDTH)
    output_sel = jnp.transpose(output_h, (1, 0, 2)).reshape(partial_rows, MODEL_WIDTH)
    lse_all, delta_all = (
        lax.all_gather(lse_h.T, "seq", axis=0, tiled=True),
        lax.all_gather(delta_h.T, "seq", axis=0, tiled=True),
    )
    local_keys_h = heads_lead(key_sel, partial_rows)
    local_values_h = heads_lead(value_sel, partial_rows)
    query_piece = lax.all_gather(query_sel, "seq", axis=0, tiled=True)
    dout_piece = lax.all_gather(dout_sel, "seq", axis=0, tiled=True)
    item_count = query_piece.shape[0]
    key_part, value_part = lax.map(
        head_keyside,
        (
            heads_lead(query_piece, item_count),
            heads_lead(dout_piece, item_count),
            lse_all.T,
            delta_all.T,
            local_keys_h,
            local_values_h,
        ),
    )
    grad_k = (
        jnp.transpose(key_part, (1, 0, 2)).reshape(partial_rows, MODEL_WIDTH).astype(jnp.bfloat16)
    )
    grad_v = (
        jnp.transpose(value_part, (1, 0, 2)).reshape(partial_rows, MODEL_WIDTH).astype(jnp.bfloat16)
    )
    attended = spread_dilated(output_sel)
    gradient_list = (grad_q, grad_k, grad_v)
    dmixed_parts = []
    for residue_index in range(DILATION_STEP):
        stacked = jnp.stack(
            [
                group_index.reshape(partial_rows, each_group, DILATION_STEP, HEAD_SIZE)[
                    :, :, residue_index, :
                ]
                for group_index in gradient_list
            ],
            axis=1,
        )
        dmixed_parts.append(
            contract_last(
                stacked.reshape(partial_rows, 3 * each_group * HEAD_SIZE),
                residue_weights[residue_index],
            )
        )
    dmixed = jnp.stack(dmixed_parts, axis=1).reshape(count_of_rows, MODEL_WIDTH)
    conv_terms = jnp.stack([jnp.sum(dmixed * near_rows[k], axis=0) for k in range(KERNEL)])
    grad_conv = lax.psum(conv_terms, "seq")
    contrib = jnp.zeros((count_of_rows + 2 * REACH, MODEL_WIDTH), jnp.float32)
    for k in range(KERNEL):
        contrib = contrib.at[local_index[k]].add(
            conv_weight[k][None, :] * dmixed * valid_mask[k][:, None]
        )
    from_above = from_behind(contrib[:REACH], "seq", -1)
    from_below = from_behind(
        contrib[REACH + count_of_rows :].astype(jnp.bfloat16), "seq", 1
    ).astype(jnp.float32)
    total = dmixed + contrib[REACH : REACH + count_of_rows]
    total = total + jnp.pad(from_below, ((0, count_of_rows - REACH), (0, 0)))
    total = total + jnp.pad(from_above, ((count_of_rows - REACH, 0), (0, 0)))
    grad_tiles = total.astype(jnp.bfloat16)
    return (attended, grad_tiles, grad_conv)


ROWS = 128
PART = ROWS // DILATION_STEP
PACKED = 48
LANES = 128
CHUNKS = MODEL_WIDTH // LANES
VMEM_BYTES = 56 * 1024 * 1024


def bf16_dot(left, right):
    return jnp.dot(left, right, preferred_element_type=jnp.float32)


def one_hot(column, positions):
    return jnp.where(column == positions, 1.0, 0.0).astype(jnp.bfloat16)


def remote(source, target, send_sem, recv_sem, peer):
    return pltpu.make_async_remote_copy(
        src_ref=source,
        dst_ref=target,
        send_sem=send_sem,
        recv_sem=recv_sem,
        device_id={"seq": peer},
        device_id_type=pl.DeviceIdType.MESH,
    )


def slide_kernel(
    n,
    tile_ref,
    dout_ref,
    weight_hbm,
    conv_ref,
    near_ref,
    attended_ref,
    tiles_ref,
    taps_ref,
    weight,
    near_pad,
    columns,
    columns_perm,
    halo,
    gathered_own,
    gathered,
    hot_own,
    hot_halo,
    back_own,
    back_halo,
    dout_perm,
    heads_out,
    heads_in,
    grads_out,
    grads_in,
    split,
    back_rows,
    tap_part,
    tap_in,
    tap_all,
    weight_sem,
    halo_s,
    halo_r,
    heads_s,
    heads_r,
    grads_s,
    grads_r,
    back_s,
    back_r,
    tap_s,
    tap_r,
    all_s,
    all_r,
):
    me = lax.axis_index("seq")
    load_weight = pltpu.make_async_copy(weight_hbm, weight, weight_sem)
    load_weight.start()

    barrier = pltpu.get_barrier_semaphore()

    @pl.loop(1, n)
    def _(step):
        pl.semaphore_signal(
            barrier,
            inc=1,
            device_id={"seq": lax.rem(me + step, n)},
            device_id_type=pl.DeviceIdType.MESH,
        )

    near = near_ref[...]
    near_pad[...] = jnp.full((LANES, ROWS), -1, jnp.int32)
    near_pad[0:KERNEL, :] = jnp.where(near >= 0, near - (me - 1) * ROWS, -1)
    columns[...] = near_pad[...].T
    for r in range(DILATION_STEP):
        columns_perm[r * PART : (r + 1) * PART, :] = columns[pl.ds(r, PART, stride=DILATION_STEP), :]
    lane = lax.broadcasted_iota(jnp.int32, (ROWS, ROWS), 1)
    row = lax.broadcasted_iota(jnp.int32, (ROWS, ROWS), 0)
    tile_of_lane = (lane % PART) * DILATION_STEP + lane // PART
    tile_of_row = (row % PART) * DILATION_STEP + row // PART
    for k in range(KERNEL):
        column = columns_perm[:, k : k + 1]
        rows = slice(k * ROWS, (k + 1) * ROWS)
        hot_own[rows, :] = one_hot(column, lane + ROWS)
        hot_halo[rows, 0:ROWS] = one_hot(column, lane)
        hot_halo[rows, ROWS : 2 * ROWS] = one_hot(column, lane + 2 * ROWS)
    to_perm = one_hot(tile_of_row, lane)
    dout_perm[...] = bf16_dot(to_perm, dout_ref[...]).astype(jnp.bfloat16)

    pl.semaphore_wait(barrier, n - 1)

    def exchange(source, target, send_sem, recv_sem):
        up = remote(source, target.at[pl.ds(0, ROWS)], send_sem.at[0], recv_sem.at[0], me + 1)
        down = remote(source, target.at[pl.ds(ROWS, ROWS)], send_sem.at[1], recv_sem.at[1], me - 1)
        return up, down

    def start_exchange(copies):
        pl.when(me < n - 1)(copies[0].start)
        pl.when(me > 0)(copies[1].start)

    def arrive_exchange(copies):
        pl.when(me > 0)(copies[0].wait_recv)
        pl.when(me < n - 1)(copies[1].wait_recv)

    def finish_exchange(copies):
        pl.when(me < n - 1)(copies[0].wait_send)
        pl.when(me > 0)(copies[1].wait_send)

    def clear_ends(target):
        @pl.when(me == 0)
        def _():
            target[0:ROWS, :] = jnp.zeros((ROWS, MODEL_WIDTH), jnp.bfloat16)

        @pl.when(me == n - 1)
        def _():
            target[ROWS : 2 * ROWS, :] = jnp.zeros((ROWS, MODEL_WIDTH), jnp.bfloat16)

    tile_copies = exchange(tile_ref, halo, halo_s, halo_r)
    start_exchange(tile_copies)
    clear_ends(halo)
    clear_ends(back_rows)
    gathered_own[...] = bf16_dot(hot_own[...], tile_ref[...])
    for h in range(HEAD_COUNT):
        r = h % DILATION_STEP
        piece = dout_perm[r * PART : (r + 1) * PART, h * HEAD_SIZE : (h + 1) * HEAD_SIZE]
        heads_out[h, PART:PACKED, 32:80] = piece[0:16]
        heads_out[h, PART:PACKED, 80:128] = piece[16:32]
    for k in range(KERNEL):
        column = columns[:, k : k + 1]
        rows = slice(k * ROWS, (k + 1) * ROWS)
        own = one_hot(column, tile_of_lane + ROWS)
        back_own[rows, 0:ROWS] = own
        back_own[rows, ROWS : 2 * ROWS] = own
        back_halo[rows, 0:ROWS] = one_hot(column, tile_of_lane)
        back_halo[rows, ROWS : 2 * ROWS] = one_hot(column, tile_of_lane + 2 * ROWS)

    arrive_exchange(tile_copies)
    gathered[...] = (gathered_own[...] + bf16_dot(hot_halo[...], halo[...])).astype(jnp.bfloat16)

    def tap_rows(k):
        return gathered[k * ROWS : (k + 1) * ROWS, :].astype(jnp.float32)

    summed = tap_rows(KERNEL // 2)
    for k in range(KERNEL):
        summed = summed + conv_ref[k : k + 1, :] * tap_rows(k)
    mixed = summed.astype(jnp.bfloat16)

    load_weight.wait()
    projected = [
        bf16_dot(mixed, weight[:, s * MODEL_WIDTH : (s + 1) * MODEL_WIDTH]).astype(jnp.bfloat16)
        for s in range(3)
    ]
    for h in range(HEAD_COUNT):
        r = h % DILATION_STEP
        q, k, v = [
            x[r * PART : (r + 1) * PART, h * HEAD_SIZE : (h + 1) * HEAD_SIZE] for x in projected
        ]
        heads_out[h, 0:PART, :] = jnp.concatenate([q, k, v[:, 0:32]], axis=1)
        heads_out[h, PART:PACKED, 0:16] = v[0:16, 32:48]
        heads_out[h, PART:PACKED, 16:32] = v[16:32, 32:48]

    other = lax.rem(me + 1, n)

    def whole(source, target, send_sem, recv_sem):
        most = pl.ds(0, n - 1)
        return remote(source.at[most], target.at[most], send_sem, recv_sem, other)

    def all_to_all(source, target, send_sem, recv_sem):
        @pl.loop(1, n)
        def _(step):
            peer = me ^ (n - step)
            remote(source.at[peer], target.at[me], send_sem, recv_sem, peer).start()

        target[me] = source[me]
        whole(source, target, send_sem, recv_sem).wait_recv()

    def finish_all_to_all(source, target, send_sem, recv_sem):
        whole(source, target, send_sem, recv_sem).wait_send()

    all_to_all(heads_out, heads_in, heads_s, heads_r)

    keys_total = n * PART
    front = heads_in[:, 0:PART, :].reshape(keys_total, LANES)
    rest = heads_in[:, PART:PACKED, :]
    q = front[:, 0:48]
    k = front[:, 48:96]
    v_tail = jnp.concatenate([rest[:, :, 0:16], rest[:, :, 16:32]], axis=1).reshape(keys_total, 16)
    v = jnp.concatenate([front[:, 96:128], v_tail], axis=1)
    do = jnp.concatenate([rest[:, :, 32:80], rest[:, :, 80:128]], axis=1).reshape(keys_total, 48)
    scale = HEAD_SIZE ** (-0.5)
    scores = contract_last(k, q) * scale
    top = jnp.max(scores, axis=0, keepdims=True)
    grown = jnp.exp(scores - top)
    prob = grown * (1.0 / jnp.sum(grown, axis=0, keepdims=True))
    prob_low = prob.astype(jnp.bfloat16)
    out_t = bf16_dot(v.T, prob_low).astype(jnp.bfloat16)
    delta = jnp.sum(
        do.T.astype(jnp.float32) * out_t.astype(jnp.float32), axis=0, keepdims=True
    )
    dprob = contract_last(v, do)
    dscore = (prob * (dprob - delta) * scale).astype(jnp.bfloat16)
    out = out_t.T
    dq = bf16_dot(k.T, dscore).astype(jnp.bfloat16).T
    dk = bf16_dot(dscore, q).astype(jnp.bfloat16)
    dv = bf16_dot(prob_low, do).astype(jnp.bfloat16)
    grads_out[:, 0:PART, :] = jnp.concatenate([out, dq, dk[:, 0:32]], axis=1).reshape(
        n, PART, LANES
    )
    dk_tail = dk[:, 32:48].reshape(n, PART, 16)
    dv_rows = dv.reshape(n, PART, HEAD_SIZE)
    grads_out[:, PART:PACKED, :] = jnp.concatenate(
        [dk_tail[:, 0:16], dk_tail[:, 16:32], dv_rows[:, 0:16], dv_rows[:, 16:32]], axis=2
    )
    all_to_all(grads_out, grads_in, grads_s, grads_r)

    blank = jnp.zeros((PART, HEAD_SIZE), jnp.bfloat16)
    grown_rows = [[], [], [], []]
    for r in range(DILATION_STEP):
        lists = [[], [], [], []]
        for h in range(HEAD_COUNT):
            if h % DILATION_STEP != r:
                for entry in lists:
                    entry.append(blank)
                continue
            x = grads_in[h, 0:PART, :]
            y = grads_in[h, PART:PACKED, :]
            lists[0].append(x[:, 0:48])
            lists[1].append(x[:, 48:96])
            tail = jnp.concatenate([y[:, 0:16], y[:, 16:32]], axis=0)
            lists[2].append(jnp.concatenate([x[:, 96:128], tail], axis=1))
            lists[3].append(jnp.concatenate([y[:, 32:80], y[:, 80:128]], axis=0))
        for s in range(4):
            grown_rows[s].append(jnp.concatenate(lists[s], axis=1))
    out_perm, dq_perm, dk_perm, dv_perm = [jnp.concatenate(x, axis=0) for x in grown_rows]
    dmixed = jnp.zeros((ROWS, MODEL_WIDTH), jnp.float32)
    for s, part in enumerate((dq_perm, dk_perm, dv_perm)):
        dmixed = dmixed + contract_last(part, weight[:, s * MODEL_WIDTH : (s + 1) * MODEL_WIDTH])
    high = dmixed.astype(jnp.bfloat16)
    split[0:ROWS, :] = high
    split[ROWS : 2 * ROWS, :] = (dmixed - high.astype(jnp.float32)).astype(jnp.bfloat16)
    back_copies = exchange(split.at[pl.ds(0, ROWS)], back_rows, back_s, back_r)

    tap_part[...] = jnp.zeros_like(tap_part)
    for k in range(KERNEL):
        term = jnp.sum(dmixed * tap_rows(k), axis=0, keepdims=True)
        for c in range(CHUNKS):
            tap_part[c, k : k + 1, :] = term[:, c * LANES : (c + 1) * LANES]
    tap_copies = [
        remote(tap_part.at[c], tap_in.at[me], tap_s.at[c], tap_r, c) for c in range(CHUNKS)
    ]
    for c in range(CHUNKS):
        pl.when(me != c)(tap_copies[c].start)
    start_exchange(back_copies)

    natural = one_hot(row, tile_of_lane)
    attended_ref[...] = bf16_dot(natural, out_perm).astype(jnp.bfloat16)
    own_back = bf16_dot(back_own[...], split[...])
    total = own_back[(KERNEL // 2) * ROWS : (KERNEL // 2 + 1) * ROWS]
    for k in range(KERNEL):
        j = KERNEL - 1 - k
        total = total + conv_ref[k : k + 1, :] * own_back[j * ROWS : (j + 1) * ROWS]

    @pl.when(me < CHUNKS)
    def _():
        tap_in[me] = tap_part[me]

        whole(tap_in, tap_in, all_s, tap_r).wait_recv()

        tap_all[me] = jnp.sum(tap_in[...], axis=0)

        @pl.loop(1, n)
        def _(step):
            peer = lax.rem(me + step, n)
            remote(tap_all.at[me], tap_all.at[me], all_s, all_r.at[me], peer).start()

    finish_exchange(tile_copies)
    finish_all_to_all(heads_out, heads_in, heads_s, heads_r)
    finish_all_to_all(grads_out, grads_in, grads_s, grads_r)
    arrive_exchange(back_copies)
    halo_back = bf16_dot(back_halo[...], back_rows[...])
    for k in range(KERNEL):
        j = KERNEL - 1 - k
        total = total + conv_ref[k : k + 1, :] * halo_back[j * ROWS : (j + 1) * ROWS]
    tiles_ref[...] = total.astype(jnp.bfloat16)

    for c in range(CHUNKS):
        pl.when(me != c)(
            remote(tap_all.at[c], tap_all.at[c], all_s, all_r.at[c], c).wait_recv
        )
    for c in range(CHUNKS):
        taps_ref[:, c * LANES : (c + 1) * LANES] = tap_all[c, 0:KERNEL, :]

    finish_exchange(back_copies)
    for c in range(CHUNKS):
        pl.when(me != c)(tap_copies[c].wait_send)

    @pl.when(me < CHUNKS)
    def _():
        whole(tap_in, tap_in, all_s, tap_r).wait_send()


def per_device_heads(n, tile_embed, grad_output, query_key_value_weight, conv_weight, neighbours):
    bf16, f32, i32 = jnp.bfloat16, jnp.float32, jnp.int32
    taps = KERNEL * ROWS
    dma = pltpu.SemaphoreType.DMA
    vmem = pl.BlockSpec(memory_space=pltpu.VMEM)
    return pl.pallas_call(
        functools.partial(slide_kernel, n),
        out_shape=(
            jax.ShapeDtypeStruct((ROWS, MODEL_WIDTH), bf16),
            jax.ShapeDtypeStruct((ROWS, MODEL_WIDTH), bf16),
            jax.ShapeDtypeStruct((KERNEL, MODEL_WIDTH), f32),
        ),
        in_specs=[vmem, vmem, pl.BlockSpec(memory_space=pl.ANY), vmem, vmem],
        out_specs=(vmem, vmem, vmem),
        scratch_shapes=[
            pltpu.VMEM(query_key_value_weight.shape, bf16),
            pltpu.VMEM((LANES, ROWS), i32),
            pltpu.VMEM((ROWS, LANES), i32),
            pltpu.VMEM((ROWS, LANES), i32),
            pltpu.VMEM((2 * ROWS, MODEL_WIDTH), bf16),
            pltpu.VMEM((taps, MODEL_WIDTH), f32),
            pltpu.VMEM((taps, MODEL_WIDTH), bf16),
            pltpu.VMEM((taps, ROWS), bf16),
            pltpu.VMEM((taps, 2 * ROWS), bf16),
            pltpu.VMEM((taps, 2 * ROWS), bf16),
            pltpu.VMEM((taps, 2 * ROWS), bf16),
            pltpu.VMEM((ROWS, MODEL_WIDTH), bf16),
            pltpu.VMEM((n, PACKED, LANES), bf16),
            pltpu.VMEM((n, PACKED, LANES), bf16),
            pltpu.VMEM((n, PACKED, LANES), bf16),
            pltpu.VMEM((n, PACKED, LANES), bf16),
            pltpu.VMEM((2 * ROWS, MODEL_WIDTH), bf16),
            pltpu.VMEM((2 * ROWS, MODEL_WIDTH), bf16),
            pltpu.VMEM((CHUNKS, 16, LANES), f32),
            pltpu.VMEM((n, 16, LANES), f32),
            pltpu.VMEM((CHUNKS, 16, LANES), f32),
            dma,
            dma((2,)),
            dma((2,)),
            dma,
            dma,
            dma,
            dma,
            dma((2,)),
            dma((2,)),
            dma((CHUNKS,)),
            dma,
            dma,
            dma((CHUNKS,)),
        ],
        compiler_params=pltpu.CompilerParams(
            collective_id=0, has_side_effects=True, vmem_limit_bytes=VMEM_BYTES
        ),
    )(tile_embed, grad_output, query_key_value_weight, conv_weight, neighbours)


def hand_on_kernel(a_ref, b_ref, c_ref, a_out, b_out, c_out):
    a_out[...] = a_ref[...]
    b_out[...] = b_ref[...]
    c_out[...] = c_ref[...]


def hand_on(*arrays):
    vmem = pl.BlockSpec(memory_space=pltpu.VMEM)
    return pl.pallas_call(
        hand_on_kernel,
        out_shape=tuple(jax.ShapeDtypeStruct(x.shape, x.dtype) for x in arrays),
        in_specs=[vmem] * 3,
        out_specs=(vmem,) * 3,
    )(*arrays)


def per_device_choice(n, tile_embed, *rest):
    if n == HEAD_COUNT and tile_embed.shape[0] == ROWS:
        return hand_on(*per_device_heads(n, tile_embed, *rest))
    return per_device(tile_embed, *rest)


def solution(mesh):
    placed = (
        P(("slide", "seq"), None),
        P(("slide", "seq"), None),
        P(),
        P(),
        P(None, ("slide", "seq")),
    )
    return jax.shard_map(
        functools.partial(per_device_choice, mesh.shape["seq"]),
        mesh=mesh,
        in_specs=placed,
        out_specs=(P(("slide", "seq"), None), P(("slide", "seq"), None), P("slide", None)),
        check_vma=False,
    )
```

```python
import functools

import jax
import jax.numpy as jnp
from jax import lax
from jax.experimental import pallas as pl
from jax.experimental.pallas import tpu as pltpu
from jax.sharding import PartitionSpec as P

MODEL_WIDTH = 768
HEAD_COUNT = 16
HEAD_SIZE = 48
DILATION_STEP = 4
KERNEL = 9
REACH = 127


def extended_2(shard, sides, width):
    for axis, dim in sides:
        count, length = (lax.axis_size(axis), shard.shape[dim])
        up = [(i, (i + 1) % count) for i in range(count - 1)]
        down = [(j, i) for i, j in up]
        last = lax.slice_in_dim(shard, length - width, length, axis=dim)
        leading = lax.slice_in_dim(shard, 0, width, axis=dim)
        before = lax.ppermute(last, axis, up)
        after = lax.ppermute(leading, axis, down)
        shard = jnp.concatenate([before, shard, after], axis=dim)
    return shard


def from_behind(value, axis, steps):
    count = lax.axis_size(axis)
    leading, last = (max(0, -steps), min(count, count - steps))
    return lax.ppermute(value, axis, [(source, source + steps) for source in range(leading, last)])


def select_dilated(full_result, item_count):
    each_group = HEAD_COUNT // DILATION_STEP
    five_value = full_result.reshape(
        item_count // DILATION_STEP, DILATION_STEP, each_group, DILATION_STEP, HEAD_SIZE
    )
    return jnp.stack(
        [
            five_value[:, residue_index, :, residue_index, :]
            for residue_index in range(DILATION_STEP)
        ],
        axis=2,
    ).reshape(item_count // DILATION_STEP, MODEL_WIDTH)


def spread_dilated(selected_rows):
    item_count = selected_rows.shape[0]
    five_value = selected_rows.reshape(
        item_count, 1, HEAD_COUNT // DILATION_STEP, DILATION_STEP, HEAD_SIZE
    )
    unit_vector = jnp.eye(DILATION_STEP, dtype=selected_rows.dtype).reshape(
        1, DILATION_STEP, 1, DILATION_STEP, 1
    )
    return (five_value * unit_vector).reshape(item_count * DILATION_STEP, MODEL_WIDTH)


def contract_last(left, right):
    return lax.dot_general(
        left, right, (((1,), (1,)), ((), ())), preferred_element_type=jnp.float32
    )


def contract_first(left, right):
    return lax.dot_general(
        left, right, (((0,), (0,)), ((), ())), preferred_element_type=jnp.float32
    )


def head_forward(items):
    queries, keys, values, douts = items
    scale = HEAD_SIZE ** (-0.5)
    scores = contract_last(queries, keys) * scale
    top = jnp.max(scores, axis=1, keepdims=True)
    log_total = top + jnp.log(jnp.sum(jnp.exp(scores - top), axis=1, keepdims=True))
    weights = jnp.exp(scores - log_total)
    weights_low = weights.astype(jnp.bfloat16)
    output = jnp.dot(weights_low, values, preferred_element_type=jnp.float32).astype(jnp.bfloat16)
    delta = jnp.sum(douts.astype(jnp.float32) * output.astype(jnp.float32), axis=1)
    dprob = contract_last(douts, values)
    dscore = (weights * (dprob - delta[:, None]) * scale).astype(jnp.bfloat16)
    grad_q = jnp.dot(dscore, keys, preferred_element_type=jnp.float32).astype(jnp.bfloat16)
    return (output, log_total[:, 0], delta, grad_q)


def head_keyside(items):
    query_piece, dout_piece, lse_piece, delta_piece, local_keys, local_values = items
    scale = HEAD_SIZE ** (-0.5)
    piece_scores = contract_last(query_piece, local_keys) * scale
    piece_weights = jnp.exp(piece_scores - lse_piece[:, None])
    value_part = contract_first(piece_weights.astype(jnp.bfloat16), dout_piece)
    piece_dprob = contract_last(dout_piece, local_values)
    piece_dscore = (piece_weights * (piece_dprob - delta_piece[:, None]) * scale).astype(
        jnp.bfloat16
    )
    key_part = contract_first(piece_dscore, query_piece)
    return (key_part, value_part)


def heads_lead(values, item_count):
    return jnp.transpose(values.reshape(item_count, HEAD_COUNT, HEAD_SIZE), (1, 0, 2))


def per_device(tile_embed, grad_output, query_key_value_weight, conv_weight, neighbours):
    count_of_rows = tile_embed.shape[0]
    partial_rows = count_of_rows // DILATION_STEP
    each_group = HEAD_COUNT // DILATION_STEP
    extended = extended_2(tile_embed, (("seq", 0),), REACH)
    valid = neighbours >= 0
    offset = lax.axis_index("seq") * count_of_rows - REACH
    local_index = jnp.where(valid, neighbours - offset, 0)
    valid_mask = valid.astype(jnp.float32)
    near_rows = [
        extended[local_index[k]].astype(jnp.float32) * valid_mask[k][:, None] for k in range(KERNEL)
    ]
    summed = tile_embed.astype(jnp.float32)
    for k in range(KERNEL):
        summed = summed + conv_weight[k][None, :] * near_rows[k]
    mixed_tiles = summed.astype(jnp.bfloat16)
    split_weights = query_key_value_weight.reshape(
        MODEL_WIDTH, 3, each_group, DILATION_STEP, HEAD_SIZE
    )
    per_residue_class = mixed_tiles.reshape(partial_rows, DILATION_STEP, MODEL_WIDTH)
    residue_weights = [
        split_weights[:, :, :, residue_index, :].reshape(MODEL_WIDTH, 3 * each_group * HEAD_SIZE)
        for residue_index in range(DILATION_STEP)
    ]
    projected = jnp.stack(
        [
            jnp.dot(
                per_residue_class[:, residue_index, :],
                residue_weights[residue_index],
                preferred_element_type=jnp.float32,
            )
            .astype(jnp.bfloat16)
            .reshape(partial_rows, 3, each_group, HEAD_SIZE)
            for residue_index in range(DILATION_STEP)
        ],
        axis=3,
    )
    query_sel = projected[:, 0].reshape(partial_rows, MODEL_WIDTH)
    key_sel = projected[:, 1].reshape(partial_rows, MODEL_WIDTH)
    value_sel = projected[:, 2].reshape(partial_rows, MODEL_WIDTH)
    dout_sel = select_dilated(grad_output, count_of_rows)
    key_all, value_all = (
        lax.all_gather(key_sel, "seq", axis=0, tiled=True),
        lax.all_gather(value_sel, "seq", axis=0, tiled=True),
    )
    total_keys = key_all.shape[0]
    output_h, lse_h, delta_h, grad_q_h = lax.map(
        head_forward,
        (
            heads_lead(query_sel, partial_rows),
            heads_lead(key_all, total_keys),
            heads_lead(value_all, total_keys),
            heads_lead(dout_sel, partial_rows),
        ),
    )
    grad_q = jnp.transpose(grad_q_h, (1, 0, 2)).reshape(partial_rows, MODEL_WIDTH)
    output_sel = jnp.transpose(output_h, (1, 0, 2)).reshape(partial_rows, MODEL_WIDTH)
    lse_all, delta_all = (
        lax.all_gather(lse_h.T, "seq", axis=0, tiled=True),
        lax.all_gather(delta_h.T, "seq", axis=0, tiled=True),
    )
    local_keys_h = heads_lead(key_sel, partial_rows)
    local_values_h = heads_lead(value_sel, partial_rows)
    query_piece = lax.all_gather(query_sel, "seq", axis=0, tiled=True)
    dout_piece = lax.all_gather(dout_sel, "seq", axis=0, tiled=True)
    item_count = query_piece.shape[0]
    key_part, value_part = lax.map(
        head_keyside,
        (
            heads_lead(query_piece, item_count),
            heads_lead(dout_piece, item_count),
            lse_all.T,
            delta_all.T,
            local_keys_h,
            local_values_h,
        ),
    )
    grad_k = (
        jnp.transpose(key_part, (1, 0, 2)).reshape(partial_rows, MODEL_WIDTH).astype(jnp.bfloat16)
    )
    grad_v = (
        jnp.transpose(value_part, (1, 0, 2)).reshape(partial_rows, MODEL_WIDTH).astype(jnp.bfloat16)
    )
    attended = spread_dilated(output_sel)
    gradient_list = (grad_q, grad_k, grad_v)
    dmixed_parts = []
    for residue_index in range(DILATION_STEP):
        stacked = jnp.stack(
            [
                group_index.reshape(partial_rows, each_group, DILATION_STEP, HEAD_SIZE)[
                    :, :, residue_index, :
                ]
                for group_index in gradient_list
            ],
            axis=1,
        )
        dmixed_parts.append(
            contract_last(
                stacked.reshape(partial_rows, 3 * each_group * HEAD_SIZE),
                residue_weights[residue_index],
            )
        )
    dmixed = jnp.stack(dmixed_parts, axis=1).reshape(count_of_rows, MODEL_WIDTH)
    conv_terms = jnp.stack([jnp.sum(dmixed * near_rows[k], axis=0) for k in range(KERNEL)])
    grad_conv = lax.psum(conv_terms, "seq")
    contrib = jnp.zeros((count_of_rows + 2 * REACH, MODEL_WIDTH), jnp.float32)
    for k in range(KERNEL):
        contrib = contrib.at[local_index[k]].add(
            conv_weight[k][None, :] * dmixed * valid_mask[k][:, None]
        )
    from_above = from_behind(contrib[:REACH], "seq", -1)
    from_below = from_behind(
        contrib[REACH + count_of_rows :].astype(jnp.bfloat16), "seq", 1
    ).astype(jnp.float32)
    total = dmixed + contrib[REACH : REACH + count_of_rows]
    total = total + jnp.pad(from_below, ((0, count_of_rows - REACH), (0, 0)))
    total = total + jnp.pad(from_above, ((count_of_rows - REACH, 0), (0, 0)))
    grad_tiles = total.astype(jnp.bfloat16)
    return (attended, grad_tiles, grad_conv)


ROWS = 128
PART = ROWS // DILATION_STEP
PACKED = 48
LANES = 128
CHUNKS = MODEL_WIDTH // LANES
VMEM_BYTES = 56 * 1024 * 1024


def bf16_dot(left, right):
    return jnp.dot(left, right, preferred_element_type=jnp.float32)


def one_hot(column, positions):
    return jnp.where(column == positions, 1.0, 0.0).astype(jnp.bfloat16)


def remote(source, target, send_sem, recv_sem, peer):
    return pltpu.make_async_remote_copy(
        src_ref=source,
        dst_ref=target,
        send_sem=send_sem,
        recv_sem=recv_sem,
        device_id={"seq": peer},
        device_id_type=pl.DeviceIdType.MESH,
    )


def slide_kernel(
    n,
    tile_hbm,
    dout_hbm,
    weight_hbm,
    conv_hbm,
    near_hbm,
    attended_ref,
    tiles_ref,
    taps_ref,
    weight,
    near_pad,
    columns,
    columns_perm,
    halo,
    gathered_own,
    gathered,
    hot_own,
    hot_halo,
    back_own,
    back_halo,
    dout_perm,
    heads_out,
    heads_in,
    grads_out,
    grads_in,
    split,
    back_rows,
    tap_part,
    tap_in,
    tap_all,
    weight_sem,
    halo_s,
    halo_r,
    heads_s,
    heads_r,
    grads_s,
    grads_r,
    back_s,
    back_r,
    tap_s,
    tap_r,
    all_s,
    all_r,
    tile_ref,
    dout_ref,
    conv_ref,
    near_ref,
    load_s,
):
    me = lax.axis_index("seq")
    load_weight = pltpu.make_async_copy(weight_hbm, weight, weight_sem)
    loads = [
        pltpu.make_async_copy(source, target, load_s.at[i])
        for i, (source, target) in enumerate(
            (
                (near_hbm, near_ref),
                (dout_hbm, dout_ref),
                (tile_hbm, tile_ref),
                (conv_hbm, conv_ref),
            )
        )
    ]

    barrier = pltpu.get_barrier_semaphore()

    @pl.loop(1, n)
    def _(step):
        pl.semaphore_signal(
            barrier,
            inc=1,
            device_id={"seq": lax.rem(me + step, n)},
            device_id_type=pl.DeviceIdType.MESH,
        )

    for load in loads:
        load.start()
    load_weight.start()
    for load in loads:
        load.wait()

    near = near_ref[...]
    near_pad[...] = jnp.full((LANES, ROWS), -1, jnp.int32)
    near_pad[0:KERNEL, :] = jnp.where(near >= 0, near - (me - 1) * ROWS, -1)
    columns[...] = near_pad[...].T
    for r in range(DILATION_STEP):
        columns_perm[r * PART : (r + 1) * PART, :] = columns[pl.ds(r, PART, stride=DILATION_STEP), :]
    lane = lax.broadcasted_iota(jnp.int32, (ROWS, ROWS), 1)
    row = lax.broadcasted_iota(jnp.int32, (ROWS, ROWS), 0)
    tile_of_lane = (lane % PART) * DILATION_STEP + lane // PART
    tile_of_row = (row % PART) * DILATION_STEP + row // PART
    for k in range(KERNEL):
        column = columns_perm[:, k : k + 1]
        rows = slice(k * ROWS, (k + 1) * ROWS)
        hot_own[rows, :] = one_hot(column, lane + ROWS)
        hot_halo[rows, 0:ROWS] = one_hot(column, lane)
        hot_halo[rows, ROWS : 2 * ROWS] = one_hot(column, lane + 2 * ROWS)
    to_perm = one_hot(tile_of_row, lane)
    dout_perm[...] = bf16_dot(to_perm, dout_ref[...]).astype(jnp.bfloat16)

    pl.semaphore_wait(barrier, n - 1)

    def exchange(source, target, send_sem, recv_sem):
        up = remote(source, target.at[pl.ds(0, ROWS)], send_sem.at[0], recv_sem.at[0], me + 1)
        down = remote(source, target.at[pl.ds(ROWS, ROWS)], send_sem.at[1], recv_sem.at[1], me - 1)
        return up, down

    def start_exchange(copies):
        pl.when(me < n - 1)(copies[0].start)
        pl.when(me > 0)(copies[1].start)

    def arrive_exchange(copies):
        pl.when(me > 0)(copies[0].wait_recv)
        pl.when(me < n - 1)(copies[1].wait_recv)

    def finish_exchange(copies):
        pl.when(me < n - 1)(copies[0].wait_send)
        pl.when(me > 0)(copies[1].wait_send)

    def clear_ends(target):
        @pl.when(me == 0)
        def _():
            target[0:ROWS, :] = jnp.zeros((ROWS, MODEL_WIDTH), jnp.bfloat16)

        @pl.when(me == n - 1)
        def _():
            target[ROWS : 2 * ROWS, :] = jnp.zeros((ROWS, MODEL_WIDTH), jnp.bfloat16)

    tile_copies = exchange(tile_ref, halo, halo_s, halo_r)
    start_exchange(tile_copies)
    clear_ends(halo)
    clear_ends(back_rows)
    gathered_own[...] = bf16_dot(hot_own[...], tile_ref[...])
    for h in range(HEAD_COUNT):
        r = h % DILATION_STEP
        piece = dout_perm[r * PART : (r + 1) * PART, h * HEAD_SIZE : (h + 1) * HEAD_SIZE]
        heads_out[h, PART:PACKED, 32:80] = piece[0:16]
        heads_out[h, PART:PACKED, 80:128] = piece[16:32]
    for k in range(KERNEL):
        column = columns[:, k : k + 1]
        rows = slice(k * ROWS, (k + 1) * ROWS)
        own = one_hot(column, tile_of_lane + ROWS)
        back_own[rows, 0:ROWS] = own
        back_own[rows, ROWS : 2 * ROWS] = own
        back_halo[rows, 0:ROWS] = one_hot(column, tile_of_lane)
        back_halo[rows, ROWS : 2 * ROWS] = one_hot(column, tile_of_lane + 2 * ROWS)

    arrive_exchange(tile_copies)
    gathered[...] = (gathered_own[...] + bf16_dot(hot_halo[...], halo[...])).astype(jnp.bfloat16)

    def tap_rows(k):
        return gathered[k * ROWS : (k + 1) * ROWS, :].astype(jnp.float32)

    summed = tap_rows(KERNEL // 2)
    for k in range(KERNEL):
        summed = summed + conv_ref[k : k + 1, :] * tap_rows(k)
    mixed = summed.astype(jnp.bfloat16)

    load_weight.wait()
    projected = [
        bf16_dot(mixed, weight[:, s * MODEL_WIDTH : (s + 1) * MODEL_WIDTH]).astype(jnp.bfloat16)
        for s in range(3)
    ]
    for h in range(HEAD_COUNT):
        r = h % DILATION_STEP
        q, k, v = [
            x[r * PART : (r + 1) * PART, h * HEAD_SIZE : (h + 1) * HEAD_SIZE] for x in projected
        ]
        heads_out[h, 0:PART, :] = jnp.concatenate([q, k, v[:, 0:32]], axis=1)
        heads_out[h, PART:PACKED, 0:16] = v[0:16, 32:48]
        heads_out[h, PART:PACKED, 16:32] = v[16:32, 32:48]

    other = lax.rem(me + 1, n)

    def whole(source, target, send_sem, recv_sem):
        most = pl.ds(0, n - 1)
        return remote(source.at[most], target.at[most], send_sem, recv_sem, other)

    def all_to_all(source, target, send_sem, recv_sem):
        @pl.loop(1, n)
        def _(step):
            peer = me ^ (n - step)
            remote(source.at[peer], target.at[me], send_sem, recv_sem, peer).start()

        target[me] = source[me]
        whole(source, target, send_sem, recv_sem).wait_recv()

    def finish_all_to_all(source, target, send_sem, recv_sem):
        whole(source, target, send_sem, recv_sem).wait_send()

    all_to_all(heads_out, heads_in, heads_s, heads_r)

    keys_total = n * PART
    front = heads_in[:, 0:PART, :].reshape(keys_total, LANES)
    rest = heads_in[:, PART:PACKED, :]
    q = front[:, 0:48]
    k = front[:, 48:96]
    v_tail = jnp.concatenate([rest[:, :, 0:16], rest[:, :, 16:32]], axis=1).reshape(keys_total, 16)
    v = jnp.concatenate([front[:, 96:128], v_tail], axis=1)
    do = jnp.concatenate([rest[:, :, 32:80], rest[:, :, 80:128]], axis=1).reshape(keys_total, 48)
    scale = HEAD_SIZE ** (-0.5)
    scores = contract_last(k, q) * scale
    top = jnp.max(scores, axis=0, keepdims=True)
    grown = jnp.exp(scores - top)
    prob = grown * (1.0 / jnp.sum(grown, axis=0, keepdims=True))
    prob_low = prob.astype(jnp.bfloat16)
    out_t = bf16_dot(v.T, prob_low).astype(jnp.bfloat16)
    delta = jnp.sum(
        do.T.astype(jnp.float32) * out_t.astype(jnp.float32), axis=0, keepdims=True
    )
    dprob = contract_last(v, do)
    dscore = (prob * (dprob - delta) * scale).astype(jnp.bfloat16)
    out = out_t.T
    dq = bf16_dot(k.T, dscore).astype(jnp.bfloat16).T
    dk = bf16_dot(dscore, q).astype(jnp.bfloat16)
    dv = bf16_dot(prob_low, do).astype(jnp.bfloat16)
    grads_out[:, 0:PART, :] = jnp.concatenate([out, dq, dk[:, 0:32]], axis=1).reshape(
        n, PART, LANES
    )
    dk_tail = dk[:, 32:48].reshape(n, PART, 16)
    dv_rows = dv.reshape(n, PART, HEAD_SIZE)
    grads_out[:, PART:PACKED, :] = jnp.concatenate(
        [dk_tail[:, 0:16], dk_tail[:, 16:32], dv_rows[:, 0:16], dv_rows[:, 16:32]], axis=2
    )
    all_to_all(grads_out, grads_in, grads_s, grads_r)

    blank = jnp.zeros((PART, HEAD_SIZE), jnp.bfloat16)
    grown_rows = [[], [], [], []]
    for r in range(DILATION_STEP):
        lists = [[], [], [], []]
        for h in range(HEAD_COUNT):
            if h % DILATION_STEP != r:
                for entry in lists:
                    entry.append(blank)
                continue
            x = grads_in[h, 0:PART, :]
            y = grads_in[h, PART:PACKED, :]
            lists[0].append(x[:, 0:48])
            lists[1].append(x[:, 48:96])
            tail = jnp.concatenate([y[:, 0:16], y[:, 16:32]], axis=0)
            lists[2].append(jnp.concatenate([x[:, 96:128], tail], axis=1))
            lists[3].append(jnp.concatenate([y[:, 32:80], y[:, 80:128]], axis=0))
        for s in range(4):
            grown_rows[s].append(jnp.concatenate(lists[s], axis=1))
    out_perm, dq_perm, dk_perm, dv_perm = [jnp.concatenate(x, axis=0) for x in grown_rows]
    dmixed = jnp.zeros((ROWS, MODEL_WIDTH), jnp.float32)
    for s, part in enumerate((dq_perm, dk_perm, dv_perm)):
        dmixed = dmixed + contract_last(part, weight[:, s * MODEL_WIDTH : (s + 1) * MODEL_WIDTH])
    high = dmixed.astype(jnp.bfloat16)
    split[0:ROWS, :] = high
    split[ROWS : 2 * ROWS, :] = (dmixed - high.astype(jnp.float32)).astype(jnp.bfloat16)
    back_copies = exchange(split.at[pl.ds(0, ROWS)], back_rows, back_s, back_r)

    tap_part[...] = jnp.zeros_like(tap_part)
    for k in range(KERNEL):
        term = jnp.sum(dmixed * tap_rows(k), axis=0, keepdims=True)
        for c in range(CHUNKS):
            tap_part[c, k : k + 1, :] = term[:, c * LANES : (c + 1) * LANES]
    tap_copies = [
        remote(tap_part.at[c], tap_in.at[me], tap_s.at[c], tap_r, c) for c in range(CHUNKS)
    ]
    for c in range(CHUNKS):
        pl.when(me != c)(tap_copies[c].start)
    start_exchange(back_copies)

    @pl.when(me < CHUNKS)
    def _():
        tap_in[me] = tap_part[me]

        whole(tap_in, tap_in, all_s, tap_r).wait_recv()

        tap_all[me] = jnp.sum(tap_in[...], axis=0)

        @pl.loop(1, n)
        def _(step):
            peer = lax.rem(me + step, n)
            remote(tap_all.at[me], tap_all.at[me], all_s, all_r.at[me], peer).start()

    natural = one_hot(row, tile_of_lane)
    attended_ref[...] = bf16_dot(natural, out_perm).astype(jnp.bfloat16)
    own_back = bf16_dot(back_own[...], split[...])
    total = own_back[(KERNEL // 2) * ROWS : (KERNEL // 2 + 1) * ROWS]
    for k in range(KERNEL):
        j = KERNEL - 1 - k
        total = total + conv_ref[k : k + 1, :] * own_back[j * ROWS : (j + 1) * ROWS]

    finish_exchange(tile_copies)
    finish_all_to_all(heads_out, heads_in, heads_s, heads_r)
    finish_all_to_all(grads_out, grads_in, grads_s, grads_r)
    arrive_exchange(back_copies)
    halo_back = bf16_dot(back_halo[...], back_rows[...])
    for k in range(KERNEL):
        j = KERNEL - 1 - k
        total = total + conv_ref[k : k + 1, :] * halo_back[j * ROWS : (j + 1) * ROWS]
    tiles_ref[...] = total.astype(jnp.bfloat16)

    for c in range(CHUNKS):
        pl.when(me != c)(
            remote(tap_all.at[c], tap_all.at[c], all_s, all_r.at[c], c).wait_recv
        )
    for c in range(CHUNKS):
        taps_ref[:, c * LANES : (c + 1) * LANES] = tap_all[c, 0:KERNEL, :]

    finish_exchange(back_copies)
    for c in range(CHUNKS):
        pl.when(me != c)(tap_copies[c].wait_send)

    @pl.when(me < CHUNKS)
    def _():
        whole(tap_in, tap_in, all_s, tap_r).wait_send()


def per_device_heads(n, tile_embed, grad_output, query_key_value_weight, conv_weight, neighbours):
    bf16, f32, i32 = jnp.bfloat16, jnp.float32, jnp.int32
    taps = KERNEL * ROWS
    dma = pltpu.SemaphoreType.DMA
    vmem = pl.BlockSpec(memory_space=pltpu.VMEM)
    return pl.pallas_call(
        functools.partial(slide_kernel, n),
        out_shape=(
            jax.ShapeDtypeStruct((ROWS, MODEL_WIDTH), bf16),
            jax.ShapeDtypeStruct((ROWS, MODEL_WIDTH), bf16),
            jax.ShapeDtypeStruct((KERNEL, MODEL_WIDTH), f32),
        ),
        in_specs=[pl.BlockSpec(memory_space=pl.ANY)] * 5,
        out_specs=(vmem, vmem, vmem),
        scratch_shapes=[
            pltpu.VMEM(query_key_value_weight.shape, bf16),
            pltpu.VMEM((LANES, ROWS), i32),
            pltpu.VMEM((ROWS, LANES), i32),
            pltpu.VMEM((ROWS, LANES), i32),
            pltpu.VMEM((2 * ROWS, MODEL_WIDTH), bf16),
            pltpu.VMEM((taps, MODEL_WIDTH), f32),
            pltpu.VMEM((taps, MODEL_WIDTH), bf16),
            pltpu.VMEM((taps, ROWS), bf16),
            pltpu.VMEM((taps, 2 * ROWS), bf16),
            pltpu.VMEM((taps, 2 * ROWS), bf16),
            pltpu.VMEM((taps, 2 * ROWS), bf16),
            pltpu.VMEM((ROWS, MODEL_WIDTH), bf16),
            pltpu.VMEM((n, PACKED, LANES), bf16),
            pltpu.VMEM((n, PACKED, LANES), bf16),
            pltpu.VMEM((n, PACKED, LANES), bf16),
            pltpu.VMEM((n, PACKED, LANES), bf16),
            pltpu.VMEM((2 * ROWS, MODEL_WIDTH), bf16),
            pltpu.VMEM((2 * ROWS, MODEL_WIDTH), bf16),
            pltpu.VMEM((CHUNKS, KERNEL, LANES), f32),
            pltpu.VMEM((n, KERNEL, LANES), f32),
            pltpu.VMEM((CHUNKS, KERNEL, LANES), f32),
            dma,
            dma((2,)),
            dma((2,)),
            dma,
            dma,
            dma,
            dma,
            dma((2,)),
            dma((2,)),
            dma((CHUNKS,)),
            dma,
            dma,
            dma((CHUNKS,)),
            pltpu.VMEM((ROWS, MODEL_WIDTH), bf16),
            pltpu.VMEM((ROWS, MODEL_WIDTH), bf16),
            pltpu.VMEM((KERNEL, MODEL_WIDTH), f32),
            pltpu.VMEM((KERNEL, ROWS), i32),
            dma((4,)),
        ],
        compiler_params=pltpu.CompilerParams(
            collective_id=0, has_side_effects=True, vmem_limit_bytes=VMEM_BYTES
        ),
    )(tile_embed, grad_output, query_key_value_weight, conv_weight, neighbours)


def hand_on_kernel(a_ref, b_ref, c_ref, a_out, b_out, c_out):
    a_out[...] = a_ref[...]
    b_out[...] = b_ref[...]
    c_out[...] = c_ref[...]


def hand_on(*arrays):
    vmem = pl.BlockSpec(memory_space=pltpu.VMEM)
    return pl.pallas_call(
        hand_on_kernel,
        out_shape=tuple(jax.ShapeDtypeStruct(x.shape, x.dtype) for x in arrays),
        in_specs=[vmem] * 3,
        out_specs=(vmem,) * 3,
    )(*arrays)


def per_device_choice(n, tile_embed, *rest):
    if n == HEAD_COUNT and tile_embed.shape[0] == ROWS:
        return hand_on(*per_device_heads(n, tile_embed, *rest))
    return per_device(tile_embed, *rest)


def solution(mesh):
    placed = (
        P(("slide", "seq"), None),
        P(("slide", "seq"), None),
        P(),
        P(),
        P(None, ("slide", "seq")),
    )
    return jax.shard_map(
        functools.partial(per_device_choice, mesh.shape["seq"]),
        mesh=mesh,
        in_specs=placed,
        out_specs=(P(("slide", "seq"), None), P(("slide", "seq"), None), P("slide", None)),
        check_vma=False,
    )
```
